256 devices in a mesh: dp: 32 (over y_lo, z, core), ctx: 8 (over y_hi, x).
Axes of the slice: x: 4, y: 4 (y_hi: 2, y_lo: 2; y = y_hi * 2 + y_lo), z: 8, core: 2. Of those that a mesh axis runs over, the one named last changes fastest.
Arguments:
- tokens: bfloat16 [32768, 8192], P(('dp', 'ctx')), may hold values from -24 to 24
- queries: bfloat16 [32768, 4096], P(('dp', 'ctx')), may hold values from -160 to 160
- rotated_key_rows: bfloat16 [32768, 512], P(('dp', 'ctx')), may hold values from -6 to 6
- upstream: bfloat16 [32768, 4096], P(('dp', 'ctx')), may hold values from -6 to 6
- value_projection_weight: bfloat16 [8192, 512], P('dp'), may hold values from -0.0625 to 0.0625
- doc_lengths: int32 [256, 4], P(('dp', 'ctx')), may hold values from 1 to 32, 64 in all within a row
- stretch_order: int32 [32, 8], P('dp'), may hold values from 0 to 7, each once within a row
Outputs:
- d_query: float32 [32768, 4096], P(('dp', 'ctx'))
- d_key: float32 [32768, 512], P(('dp', 'ctx'))
- weight_grad: float32 [8192, 512], P('dp')
The draws below stay inside these ranges and needn't reach their ends.
Inputs may be any that keep to these rules, and one draw needn't show every extreme that they name: `doc_lengths`: each row is the lengths of the 4 short documents of one device, summing to 64; its largest is exactly 32. `stretch_order`: each row is a permutation of the block numbers of one pack's long document.
All inputs are finite; a program needn't handle non-finite values.
Results may differ from the reference program's by a relative error of at most 0.0055.
Values may be sent and summed in bfloat16 or wider, within the bound.
No kernel may reach another device: no remote copies, remote signals or barrier semaphores. Data moves between devices by JAX's collectives and lax.ppermute only.
A program may use at most 128 MiB of HBM per device.

```python
import math
import jax
import jax.numpy as jnp
import numpy as np
from jax import lax

MODEL_WIDTH = 8192
QUERY_HEADS = 32
KEY_VALUE_HEADS = 4
HEAD_SIZE = 128
LB = 64
SB = 64
S_DOCS = 4
SMOST = 32
TOK_DEV = 128
TOKEN_TOTAL = 32768
N_DP = 32
N_CTX = 8


def key_base(key):
    return jnp.clip(jax.random.normal(key, (TOKEN_TOTAL, KEY_VALUE_HEADS * HEAD_SIZE), jnp.float32), -6.0, 6.0)


def draw_rotated_key_rows(key, part):
    base_offset = key_base(key)
    return base_offset.astype(jnp.bfloat16)


def draw_queries(key, part):
    key = jax.random.fold_in(key, 7)
    fresh = jnp.clip(jax.random.normal(key, (TOKEN_TOTAL, QUERY_HEADS * HEAD_SIZE), jnp.float32), -6.0, 6.0)
    return fresh.astype(jnp.bfloat16)


def strengthened(drawn, stream_key, source, target, shards_of, factor):
    def block_of(axis_at):
        return (jnp.arange(drawn.shape[axis_at]) // (drawn.shape[axis_at] // shards_of)).reshape((-1,) + (1,) * (drawn.ndim - 1 - axis_at))

    near = jax.random.permutation(stream_key, shards_of)[block_of(target)]
    other_side = (block_of(target) + shards_of // 2) % shards_of
    return jnp.where((block_of(source) == near) | (block_of(source) == other_side), factor * drawn, drawn)


def steps_of(key, shape, cuts, smallest, high):
    loudness, own = 1.0, jax.random.fold_in(key, 6)
    for dim, blocks in cuts:
        draws = jnp.exp(jax.random.uniform(jax.random.fold_in(own, dim), (blocks,), jnp.float32, smallest / len(cuts), high / len(cuts)))
        loudness = loudness * jnp.repeat(draws, shape[dim] // blocks).reshape([-1 if axis == dim else 1 for axis in range(len(shape))])
    return loudness


def profile(count, total, limit, skew):
    loads = [(1 << 20) // math.isqrt(grade ** skew) + 1 for grade in range(2, count + 1)]
    spare, given = total - limit - (count - 1), [1] * (count - 1)
    while spare > 0:
        movable = [i for i in range(count - 1) if given[i] < limit]
        pool, remaining = sum([loads[i] for i in movable]), spare
        for i in movable:
            addition = min(limit - given[i], max(1, remaining * loads[i] // pool), spare)
            given[i] = given[i] + addition
            spare = spare - addition
    return np.array([limit] + given)


def uneven_parts(key, number_of, total, bound, lean):
    if number_of == 2:
        one = jax.random.randint(key, (), max(1, total - bound), min(bound, total - 1) + 1)
        return jnp.stack([one, total - one])
    sizes = jnp.asarray(profile(number_of, total, bound, lean), jnp.int32)
    twos = (number_of - 1) // 2
    source_of, receiver = sizes[1:1 + 2 * twos:2], sizes[2:2 + 2 * twos:2]
    margin = jnp.minimum(source_of - 1, bound - receiver)
    passed = jax.random.randint(jax.random.fold_in(key, 1), (twos,), 0, 1 << 20) % (margin + 1)
    sizes = sizes.at[1:1 + 2 * twos:2].set(source_of - passed).at[2:2 + 2 * twos:2].set(receiver + passed)
    return sizes[jax.random.permutation(jax.random.fold_in(key, 2), number_of)]


def noise(own_key, shape, width, bound, cuts=(), kind=jnp.bfloat16):
    gain = steps_of(own_key, shape, cuts, -0.22, 0.18) if cuts else 1.0
    values = jax.random.normal(own_key, shape, jnp.float32) * width * gain
    return jnp.minimum(jnp.maximum(values, -bound), bound).astype(kind)


def heavy_noise(own_key, dims, scale, limit, cuts, heavy, kind=jnp.bfloat16):
    entries = scale * jax.random.normal(own_key, dims, jnp.float32)
    if cuts:
        entries = entries * steps_of(own_key, dims, cuts, -0.22, 0.18)
    return jnp.clip(strengthened(entries, jax.random.fold_in(own_key, 3), *heavy), -limit, limit).astype(kind)


def setup_inputs(seed: int = 0) -> dict:
    seeds = jax.random.split(jax.random.key(seed), 8)
    tokens = heavy_noise(seeds[0], (TOKEN_TOTAL, MODEL_WIDTH), 1.0, 24.0, ((0, 256),), (0, 1, 256, 6.0))
    queries = draw_queries(jax.random.fold_in(seeds[7], 71), 0)
    rotated_key_rows = draw_rotated_key_rows(jax.random.fold_in(seeds[7], 71), 0)
    upstream = noise(seeds[3], (TOKEN_TOTAL, QUERY_HEADS * HEAD_SIZE), 1.0, 6.0, ((0, 256),))
    value_projection_weight = noise(seeds[4], (MODEL_WIDTH, KEY_VALUE_HEADS * HEAD_SIZE), MODEL_WIDTH ** -0.5, 0.0625, ((0, 32),))
    doc_lengths = jax.vmap(lambda own: uneven_parts(own, S_DOCS, SB, SMOST, 2))(jax.random.split(seeds[5], (N_DP * N_CTX))).reshape((N_DP * N_CTX, S_DOCS)).astype(jnp.int32)
    stretch_order = jax.vmap(lambda own: jax.random.permutation(own, N_CTX))(jax.random.split(seeds[6], N_DP)).reshape((N_DP, N_CTX)).astype(jnp.int32)
    return dict(tokens=tokens, queries=queries, rotated_key_rows=rotated_key_rows, upstream=upstream, value_projection_weight=value_projection_weight, doc_lengths=doc_lengths, stretch_order=stretch_order)


def attend(query_matrix, upstream, rotated_key_rows, projected_value_rows, allowed):
    scale = HEAD_SIZE ** -0.5
    query_count = query_matrix.shape[0]
    key_count = rotated_key_rows.shape[0]
    query_heads = query_matrix.astype(jnp.float32).reshape(query_count, KEY_VALUE_HEADS, QUERY_HEADS // KEY_VALUE_HEADS, HEAD_SIZE)
    upstream_heads = upstream.astype(jnp.float32).reshape(query_count, KEY_VALUE_HEADS, QUERY_HEADS // KEY_VALUE_HEADS, HEAD_SIZE)
    key_heads = rotated_key_rows.astype(jnp.float32).reshape(key_count, KEY_VALUE_HEADS, HEAD_SIZE)
    value_heads = projected_value_rows.astype(jnp.float32).reshape(key_count, KEY_VALUE_HEADS, HEAD_SIZE)
    scores = jnp.einsum("nkgd,mkd->kgnm", query_heads, key_heads) * scale
    scores = jnp.where(allowed, scores, -1e30)
    peak = jnp.max(scores, axis=-1, keepdims=True)
    raised = jnp.where(allowed, jnp.exp(scores - peak), 0.0)
    prob = raised / jnp.sum(raised, axis=-1, keepdims=True)
    d_prob = jnp.einsum("nkgd,mkd->kgnm", upstream_heads, value_heads)
    delta = jnp.sum(prob * d_prob, axis=-1, keepdims=True)
    d_score = lax.optimization_barrier((prob * (d_prob - delta)).astype(jnp.bfloat16)).astype(jnp.float32)
    d_query = jnp.einsum("kgnm,mkd->nkgd", d_score, key_heads).reshape(query_count, -1) * scale
    d_key = jnp.einsum("kgnm,nkgd->mkd", d_score, query_heads).reshape(key_count, -1) * scale
    prob_round = lax.optimization_barrier(prob.astype(jnp.bfloat16)).astype(jnp.float32)
    d_value = jnp.einsum("kgnm,nkgd->mkd", prob_round, upstream_heads).reshape(key_count, -1)
    return d_query, d_key, d_value


def reference(tokens, queries, rotated_key_rows, upstream, value_projection_weight, doc_lengths, stretch_order):
    values = jnp.dot(tokens, value_projection_weight, preferred_element_type=jnp.float32).astype(jnp.bfloat16)
    q_dev = queries.reshape(N_DP, N_CTX, TOK_DEV, -1)
    u_dev = upstream.reshape(N_DP, N_CTX, TOK_DEV, -1)
    k_dev = rotated_key_rows.reshape(N_DP, N_CTX, TOK_DEV, -1)
    v_dev = values.reshape(N_DP, N_CTX, TOK_DEV, -1)

    def long_pack(pieces):
        q_p, u_p, k_p, v_p, order_p = pieces
        positions = (order_p[:, None] * LB + jnp.arange(LB, dtype=jnp.int32)[None, :]).reshape(-1)
        allowed = positions[None, :] <= positions[:, None]
        return attend(q_p.reshape(N_CTX * LB, -1), u_p.reshape(N_CTX * LB, -1),
                      k_p.reshape(N_CTX * LB, -1), v_p.reshape(N_CTX * LB, -1), allowed)

    long_q, long_k, long_v = lax.map(long_pack, (q_dev[:, :, :LB], u_dev[:, :, :LB], k_dev[:, :, :LB], v_dev[:, :, :LB], stretch_order))

    def short_device(pieces):
        q_s, u_s, k_s, v_s, lengths = pieces
        doc_ends = jnp.cumsum(lengths)
        positions = jnp.arange(SB, dtype=jnp.int32)
        segment = jnp.sum((positions[:, None] >= doc_ends[None, :]).astype(jnp.int32), axis=1)
        allowed = (segment[:, None] == segment[None, :]) & (positions[None, :] <= positions[:, None])
        return attend(q_s, u_s, k_s, v_s, allowed)

    flat = N_DP * N_CTX
    short_q, short_k, short_v = lax.map(short_device, (q_dev[:, :, LB:].reshape(flat, SB, -1), u_dev[:, :, LB:].reshape(flat, SB, -1),
                                                       k_dev[:, :, LB:].reshape(flat, SB, -1), v_dev[:, :, LB:].reshape(flat, SB, -1), doc_lengths))

    def join(long_part, short_part):
        return jnp.concatenate([long_part.reshape(N_DP, N_CTX, LB, -1), short_part.reshape(N_DP, N_CTX, SB, -1)], axis=2).reshape(TOKEN_TOTAL, -1)

    d_query = join(long_q, short_q)
    d_key = join(long_k, short_k)
    d_value = join(long_v, short_v).astype(jnp.bfloat16)
    weight_grad = jnp.dot(tokens.T, d_value, preferred_element_type=jnp.float32)
    return d_query, d_key, weight_grad
```

```python
import functools
import math

import jax
import jax.numpy as jnp
from jax import lax
from jax.experimental import pallas as pl
from jax.experimental.pallas import tpu as pltpu
from jax.sharding import Mesh
from jax.sharding import PartitionSpec as P

QUERY_HEADS = 32
KEY_VALUE_HEADS = 4
HEAD_SIZE = 128
GROUP = QUERY_HEADS // KEY_VALUE_HEADS
LB = 64
SB = 64
S_DOCS = 4
N_CTX = 8
CHUNK = 4
LANES = CHUNK * LB
SCALE = HEAD_SIZE ** -0.5
NEG = -1e30


def fill_masks(order_ref, place_ref, ends_ref, long_bias, short_bias):
    key = lax.broadcasted_iota(jnp.int32, (LB, LANES), 0)
    query = lax.broadcasted_iota(jnp.int32, (LB, LANES), 1) & (LB - 1)
    mine = place_ref[0]
    for block in range(N_CTX):
        ahead = order_ref[block] * LB + key <= mine * LB + query
        long_bias[pl.ds(block * LB, LB), :] = jnp.where(ahead, 0.0, NEG)
    key_doc = jnp.zeros((SB, LANES), jnp.int32)
    query_doc = jnp.zeros((SB, LANES), jnp.int32)
    for doc in range(S_DOCS):
        key_doc += (key >= ends_ref[doc]).astype(jnp.int32)
        query_doc += (query >= ends_ref[doc]).astype(jnp.int32)
    short_bias[...] = jnp.where((key_doc == query_doc) & (key <= query), 0.0, NEG)


def head_rows(ref, first, at):
    return jnp.concatenate(
        [ref[first:first + LB, (at + g) * HEAD_SIZE:(at + g + 1) * HEAD_SIZE] for g in range(CHUNK)],
        axis=0,
    )


def probs(keys, q_rows, bias):
    s = lax.dot_general(keys, q_rows, (((1,), (1,)), ((), ())), preferred_element_type=jnp.float32)
    s = s * (SCALE * math.log2(math.e)) + bias
    e = jnp.exp2(s - jnp.max(s, axis=0, keepdims=True))
    return e * (1.0 / jnp.sum(e, axis=0, keepdims=True))


def stacked(refs):
    return jnp.concatenate([ref[...] for ref in refs], axis=0)


def unstack(value, refs):
    for block, ref in enumerate(refs):
        ref[...] = value[block * LB:(block + 1) * LB].astype(ref.dtype)


def dvalue_kernel(order_ref, place_ref, ends_ref, slot_ref, q_ref, u_ref, ks_ref, *refs):
    k_refs, dvl_refs = refs[:N_CTX], refs[N_CTX:2 * N_CTX]
    dvs_ref, long_bias, short_bias = refs[2 * N_CTX:]

    @pl.when(pl.program_id(0) == 0)
    def _():
        fill_masks(order_ref, place_ref, ends_ref, long_bias, short_bias)

    for first, keys, bias, out in (
        (0, stacked(k_refs), long_bias, dvl_refs),
        (LB, ks_ref[LB:, :], short_bias, [dvs_ref]),
    ):
        total = None
        for at in range(0, GROUP, CHUNK):
            p = probs(keys, head_rows(q_ref, first, at), bias[...]).astype(jnp.bfloat16)
            part = jnp.dot(p, head_rows(u_ref, first, at), preferred_element_type=jnp.float32)
            total = part if total is None else total + part
        unstack(total, out)


def dscore_kernel(order_ref, place_ref, ends_ref, slot_ref, q_ref, u_ref, ks_ref, vs_ref, *refs):
    k_refs, v_refs = refs[:N_CTX], refs[N_CTX:2 * N_CTX]
    dq_ref, *dkl_refs = refs[2 * N_CTX:3 * N_CTX + 1]
    dks_ref, long_bias, short_bias = refs[3 * N_CTX + 1:]

    @pl.when(pl.program_id(0) == 0)
    def _():
        fill_masks(order_ref, place_ref, ends_ref, long_bias, short_bias)

    for first, keys, values, bias, out in (
        (0, stacked(k_refs), stacked(v_refs), long_bias, dkl_refs),
        (LB, ks_ref[LB:, :], vs_ref[LB:, :], short_bias, [dks_ref]),
    ):
        total = None
        for at in range(0, GROUP, CHUNK):
            q_rows = head_rows(q_ref, first, at)
            p = probs(keys, q_rows, bias[...])
            dp = lax.dot_general(values, head_rows(u_ref, first, at), (((1,), (1,)), ((), ())),
                                 preferred_element_type=jnp.float32)
            delta = jnp.sum(p * dp, axis=0, keepdims=True)
            ds = (p * (dp - delta)).astype(jnp.bfloat16)
            part = jnp.dot(ds, q_rows, preferred_element_type=jnp.float32)
            total = part if total is None else total + part
            dq = lax.dot_general(ds, keys, (((0,), (0,)), ((), ())),
                                 preferred_element_type=jnp.float32) * SCALE
            for g in range(CHUNK):
                dq_ref[first:first + LB, (at + g) * HEAD_SIZE:(at + g + 1) * HEAD_SIZE] = (
                    dq[g * LB:(g + 1) * LB])
        unstack(total * SCALE, out)


WIDE = GROUP * HEAD_SIZE


def block(rows, columns):
    return pl.BlockSpec((rows, columns), lambda k, *_: (0, k))


def slot_block(slot):
    return pl.BlockSpec((LB, HEAD_SIZE), lambda k, *scalars: (scalars[3][slot], k))


def scratch():
    return [pltpu.VMEM((N_CTX * LB, LANES), jnp.float32), pltpu.VMEM((SB, LANES), jnp.float32)]


def dvalues(scalars, queries, upstream, keys, all_keys, kind):
    tok = LB + SB
    long_rows = jax.ShapeDtypeStruct((LB, KEY_VALUE_HEADS * HEAD_SIZE), kind)
    out = pl.pallas_call(
        dvalue_kernel,
        grid_spec=pltpu.PrefetchScalarGridSpec(
            num_scalar_prefetch=4,
            grid=(KEY_VALUE_HEADS,),
            in_specs=[block(tok, WIDE)] * 2 + [block(tok, HEAD_SIZE)]
            + [slot_block(s) for s in range(N_CTX)],
            out_specs=[block(LB, HEAD_SIZE)] * N_CTX + [block(SB, HEAD_SIZE)],
            scratch_shapes=scratch(),
        ),
        out_shape=[long_rows] * N_CTX
        + [jax.ShapeDtypeStruct((SB, KEY_VALUE_HEADS * HEAD_SIZE), jnp.bfloat16)],
        compiler_params=pltpu.CompilerParams(vmem_limit_bytes=32 << 20),
        cost_estimate=pl.CostEstimate(flops=700_000_000, bytes_accessed=4 << 20, transcendentals=1 << 20),
    )(*scalars, queries, upstream, keys, *[all_keys] * N_CTX)
    return out[:N_CTX], out[N_CTX]


def dscores(scalars, queries, upstream, keys, values, all_keys, value_blocks, kind):
    tok = LB + SB
    long_rows = jax.ShapeDtypeStruct((LB, KEY_VALUE_HEADS * HEAD_SIZE), kind)
    out = pl.pallas_call(
        dscore_kernel,
        grid_spec=pltpu.PrefetchScalarGridSpec(
            num_scalar_prefetch=4,
            grid=(KEY_VALUE_HEADS,),
            in_specs=[block(tok, WIDE)] * 2 + [block(tok, HEAD_SIZE)] * 2
            + [slot_block(s) for s in range(N_CTX)] + [block(LB, HEAD_SIZE)] * N_CTX,
            out_specs=[block(tok, WIDE)] + [block(LB, HEAD_SIZE)] * N_CTX + [block(SB, HEAD_SIZE)],
            scratch_shapes=scratch(),
        ),
        out_shape=[jax.ShapeDtypeStruct((tok, QUERY_HEADS * HEAD_SIZE), jnp.float32)]
        + [long_rows] * N_CTX
        + [jax.ShapeDtypeStruct((SB, KEY_VALUE_HEADS * HEAD_SIZE), jnp.float32)],
        compiler_params=pltpu.CompilerParams(vmem_limit_bytes=32 << 20),
        cost_estimate=pl.CostEstimate(flops=1_400_000_000, bytes_accessed=6 << 20, transcendentals=1 << 20),
    )(*scalars, queries, upstream, keys, values, *[all_keys] * N_CTX, *value_blocks)
    return out[0], out[1:1 + N_CTX], out[1 + N_CTX]


Y_LO, CORES = 2, 2
DP = ("ylo", "z", "core")
CTX = ("yhi", "x")


PIECE = 32
DP_BLOCK = N_CTX * PIECE
TOGETHER = 4


def whole(count=1):
    return [pl.BlockSpec(memory_space=pltpu.VMEM)] * count


def regroup_kernel(me_ref, *refs):
    *block_refs, out_ref = refs
    for member in range(N_CTX):
        out_ref[member] = jnp.concatenate(
            [ref[:, member * PIECE:(member + 1) * PIECE] for ref in block_refs], axis=1)


def regroup(me, tokens):
    rows, width = tokens.shape
    depth = width // (DP_BLOCK * Y_LO * CORES)

    def source(at):
        def index(g, me_ref):
            slot = g * TOGETHER + at
            core, y_lo, z = slot // (Y_LO * depth), slot // depth % Y_LO, slot % depth
            return 0, ((y_lo * depth + z) * CORES + core) ^ me_ref[0]
        return pl.BlockSpec((rows, DP_BLOCK), index)

    return pl.pallas_call(
        regroup_kernel,
        grid_spec=pltpu.PrefetchScalarGridSpec(
            num_scalar_prefetch=1,
            grid=(width // (DP_BLOCK * TOGETHER),),
            in_specs=[source(at) for at in range(TOGETHER)],
            out_specs=pl.BlockSpec((N_CTX, rows, PIECE * TOGETHER), lambda g, *_: (0, 0, g)),
        ),
        out_shape=jax.ShapeDtypeStruct((N_CTX, rows, width // N_CTX), tokens.dtype),
        cost_estimate=pl.CostEstimate(flops=0, bytes_accessed=4 << 20, transcendentals=0),
    )(me[None], *[tokens] * TOGETHER)


def values_kernel(slot_ref, tokens_ref, mine_ref, theirs_ref, *refs):
    *out_refs, total = refs
    rows, columns = out_refs[0].shape
    weight = jnp.concatenate([mine_ref[...], theirs_ref[...]], axis=0)
    for first in range(0, total.shape[0], 2 * rows):
        total[first:first + 2 * rows] = jnp.dot(
            tokens_ref[first:first + 2 * rows], weight, preferred_element_type=jnp.float32)
    for slot, ref in enumerate(out_refs):
        start = pl.multiple_of(slot_ref[slot] * rows, rows)
        ref[...] = total[pl.ds(start, rows), :].astype(ref.dtype)


def value_parts(slots, tokens, mine, theirs):
    rows, columns = tokens.shape[0] // N_CTX, mine.shape[1]
    return pl.pallas_call(
        values_kernel,
        in_specs=[pl.BlockSpec(memory_space=pltpu.SMEM)] + whole(3),
        out_specs=whole(N_CTX),
        out_shape=[jax.ShapeDtypeStruct((rows, columns), jnp.bfloat16)] * N_CTX,
        scratch_shapes=[pltpu.VMEM((tokens.shape[0], columns), jnp.float32)],
        compiler_params=pltpu.CompilerParams(vmem_limit_bytes=32 << 20),
        cost_estimate=pl.CostEstimate(flops=2 * tokens.size * columns, bytes_accessed=4 << 20,
                                      transcendentals=0),
    )(slots, tokens, mine, theirs)


def weight_kernel(half, me_ref, tokens_ref, d_value_ref, *refs):
    *add_refs, out_ref = refs
    count, rows, columns = out_ref.shape
    some = min(DP_BLOCK // PIECE, count)
    for first in range(0, count, some):
        at = (half * count + first) * rows
        part = lax.dot_general(
            tokens_ref[:, at:at + some * rows], d_value_ref[...], (((0,), (0,)), ((), ())),
            preferred_element_type=jnp.float32)
        for slot in range(some):
            block = (first + slot) ^ me_ref[0]
            piece = part[slot * rows:(slot + 1) * rows]
            for ref in add_refs:
                piece += ref[block].astype(jnp.float32)
            out_ref[block] = piece.astype(out_ref.dtype)


def weight_share(half, me, tokens, d_value, *added):
    count, columns = tokens.shape[1] // (CORES * PIECE), d_value.shape[1]
    return pl.pallas_call(
        functools.partial(weight_kernel, half),
        in_specs=[pl.BlockSpec(memory_space=pltpu.SMEM)] + whole(2 + len(added)),
        out_specs=whole()[0],
        out_shape=jax.ShapeDtypeStruct((count, PIECE, columns), jnp.bfloat16),
        compiler_params=pltpu.CompilerParams(vmem_limit_bytes=32 << 20),
        cost_estimate=pl.CostEstimate(flops=tokens.size * columns, bytes_accessed=3 << 20,
                                      transcendentals=0),
    )(me[None], tokens, d_value, *added)


def exchange(pieces, axes):
    return lax.all_to_all(pieces, axes, 0, 0, tiled=True)


def spread(piece, axes):
    count = lax.axis_size(axes)
    return exchange(jnp.broadcast_to(piece[None], (count,) + piece.shape), axes)


def swap(array, step):
    return lax.ppermute(array, CTX, [(i, i ^ step) for i in range(N_CTX)]) if step else array


def total_kernel(pieces_ref, out_ref):
    total = pieces_ref[0].astype(jnp.float32)
    for piece in range(1, pieces_ref.shape[0]):
        total += pieces_ref[piece].astype(jnp.float32)
    out_ref[...] = total.astype(out_ref.dtype)


def total_of(pieces, kind):
    return pl.pallas_call(
        total_kernel,
        in_specs=[pl.BlockSpec(memory_space=pltpu.VMEM)],
        out_specs=pl.BlockSpec(memory_space=pltpu.VMEM),
        out_shape=jax.ShapeDtypeStruct(pieces.shape[1:], kind),
        cost_estimate=pl.CostEstimate(flops=pieces.size, bytes_accessed=2 * pieces.size, transcendentals=0),
    )(pieces)


def swap_along(array, axis, step):
    count = lax.axis_size(axis)
    return lax.ppermute(array, axis, [(i, i ^ step) for i in range(count)])


def on_device(tokens, queries, rotated_key_rows, upstream, value_projection_weight, doc_lengths,
              stretch_order):
    width = KEY_VALUE_HEADS * HEAD_SIZE
    tok_dev = LB + SB
    member = lax.axis_index(CTX)
    plane = lax.axis_index(("ylo", "z"))
    slots = member ^ jnp.arange(N_CTX, dtype=jnp.int32)
    order = jnp.take(stretch_order[0], slots)
    scalars = (order, order[:1], jnp.cumsum(doc_lengths[0]), slots)

    all_keys = spread(rotated_key_rows[:LB], CTX).reshape(N_CTX * LB, width)
    grouped = regroup(plane * CORES + lax.axis_index("core"), tokens)
    grouped, all_keys = lax.optimization_barrier((grouped, all_keys))
    tok = exchange(grouped, CTX).reshape(N_CTX * tok_dev, -1)

    dv_parts, dv_short = dvalues(scalars, queries, upstream, rotated_key_rows, all_keys, jnp.bfloat16)
    dv_long = sum(swap(dv_parts[s], s).astype(jnp.float32) for s in range(N_CTX)).astype(jnp.bfloat16)

    weight = lax.dynamic_slice_in_dim(value_projection_weight, member * PIECE, PIECE, 0)
    weight, _ = lax.optimization_barrier((weight, grouped))
    step = 1
    while step < lax.axis_size("z"):
        weight = jnp.concatenate([weight, swap_along(weight, "z", step)], axis=0)
        step *= 2
    weight = jnp.concatenate([weight, swap_along(weight, "ylo", 1)], axis=0)
    other_weight = swap_along(weight, "core", 1)

    d_value = jnp.concatenate([dv_long, dv_short], axis=0)
    d_value, tok, weight, other_weight = lax.optimization_barrier((d_value, tok, weight, other_weight))
    d_value = spread(d_value, CTX).reshape(N_CTX * tok_dev, width)
    parts = value_parts(slots, tok, weight, other_weight)
    values = sum(swap(parts[s], s).astype(jnp.float32) for s in range(N_CTX)).astype(jnp.bfloat16)

    share = swap_along(weight_share(1, plane, tok, d_value), "core", 1)
    share = weight_share(0, plane, tok, d_value, share)
    share, values = lax.optimization_barrier((share, values))
    share = exchange(share, ("ylo", "z"))
    value_blocks = [swap(values[:LB], s) for s in range(N_CTX)]
    share = total_of(share, jnp.bfloat16)
    share, value_blocks = lax.optimization_barrier((share, value_blocks))
    weight_grad = spread(share, CTX).reshape(DP_BLOCK, width).astype(jnp.float32)
    d_query, dk_parts, dk_short = dscores(scalars, queries, upstream, rotated_key_rows, values,
                                          all_keys, value_blocks, jnp.bfloat16)
    dk_long = sum(swap(dk_parts[s], s).astype(jnp.float32) for s in range(N_CTX))
    d_key = jnp.concatenate([dk_long, dk_short], axis=0)
    return d_query, d_key, weight_grad


def solution(mesh):
    packs = mesh.shape["dp"]
    mesh = Mesh(mesh.devices.reshape(Y_LO, packs // (Y_LO * CORES), CORES, 2, N_CTX // 2), DP + CTX)
    rows = P(DP + CTX, None)
    return jax.shard_map(
        on_device,
        mesh=mesh,
        in_specs=(rows, rows, rows, rows, P(DP, None), rows, P(DP, None)),
        out_specs=(rows, rows, P(DP, None)),
        check_vma=False,
    )
```

```python
import functools
import math

import jax
import jax.numpy as jnp
from jax import lax
from jax.experimental import pallas as pl
from jax.experimental.pallas import tpu as pltpu
from jax.sharding import Mesh
from jax.sharding import PartitionSpec as P

QUERY_HEADS = 32
KEY_VALUE_HEADS = 4
HEAD_SIZE = 128
GROUP = QUERY_HEADS // KEY_VALUE_HEADS
LB = 64
SB = 64
S_DOCS = 4
N_CTX = 8
CHUNK = 4
LANES = CHUNK * LB
SCALE = HEAD_SIZE ** -0.5
NEG = -1e30


def fill_masks(order_ref, place_ref, ends_ref, long_bias, short_bias):
    key = lax.broadcasted_iota(jnp.int32, (LB, LANES), 0)
    query = lax.broadcasted_iota(jnp.int32, (LB, LANES), 1) & (LB - 1)
    mine = place_ref[0]
    for block in range(N_CTX):
        ahead = order_ref[block] * LB + key <= mine * LB + query
        long_bias[pl.ds(block * LB, LB), :] = jnp.where(ahead, 0.0, NEG)
    key_doc = jnp.zeros((SB, LANES), jnp.int32)
    query_doc = jnp.zeros((SB, LANES), jnp.int32)
    for doc in range(S_DOCS):
        key_doc += (key >= ends_ref[doc]).astype(jnp.int32)
        query_doc += (query >= ends_ref[doc]).astype(jnp.int32)
    short_bias[...] = jnp.where((key_doc == query_doc) & (key <= query), 0.0, NEG)


def head_rows(ref, first, at):
    return jnp.concatenate(
        [ref[first:first + LB, (at + g) * HEAD_SIZE:(at + g + 1) * HEAD_SIZE] for g in range(CHUNK)],
        axis=0,
    )


def probs(keys, q_rows, bias):
    s = lax.dot_general(keys, q_rows, (((1,), (1,)), ((), ())), preferred_element_type=jnp.float32)
    s = s * (SCALE * math.log2(math.e)) + bias
    e = jnp.exp2(s - jnp.max(s, axis=0, keepdims=True))
    return e * (1.0 / jnp.sum(e, axis=0, keepdims=True))


def dvalue_kernel(order_ref, place_ref, ends_ref, q_ref, u_ref, ks_ref, k_ref,
                  dvl_ref, dvs_ref, long_bias, short_bias):
    @pl.when(pl.program_id(0) == 0)
    def _():
        fill_masks(order_ref, place_ref, ends_ref, long_bias, short_bias)

    for first, keys, bias, out in (
        (0, k_ref[...].reshape(N_CTX * LB, HEAD_SIZE), long_bias, dvl_ref),
        (LB, ks_ref[LB:, :], short_bias, dvs_ref),
    ):
        total = None
        for at in range(0, GROUP, CHUNK):
            p = probs(keys, head_rows(q_ref, first, at), bias[...]).astype(jnp.bfloat16)
            part = jnp.dot(p, head_rows(u_ref, first, at), preferred_element_type=jnp.float32)
            total = part if total is None else total + part
        out[...] = total.astype(out.dtype).reshape(out.shape)


def dscore_kernel(order_ref, place_ref, ends_ref, q_ref, u_ref, ks_ref, vs_ref, k_ref, v_ref,
                  dq_ref, dkl_ref, dks_ref, long_bias, short_bias):
    @pl.when(pl.program_id(0) == 0)
    def _():
        fill_masks(order_ref, place_ref, ends_ref, long_bias, short_bias)

    long_shape = (N_CTX * LB, HEAD_SIZE)
    for first, keys, values, bias, out in (
        (0, k_ref[...].reshape(long_shape), v_ref[...].reshape(long_shape), long_bias, dkl_ref),
        (LB, ks_ref[LB:, :], vs_ref[LB:, :], short_bias, dks_ref),
    ):
        total = None
        for at in range(0, GROUP, CHUNK):
            q_rows = head_rows(q_ref, first, at)
            p = probs(keys, q_rows, bias[...])
            dp = lax.dot_general(values, head_rows(u_ref, first, at), (((1,), (1,)), ((), ())),
                                 preferred_element_type=jnp.float32)
            delta = jnp.sum(p * dp, axis=0, keepdims=True)
            ds = (p * (dp - delta)).astype(jnp.bfloat16)
            part = jnp.dot(ds, q_rows, preferred_element_type=jnp.float32)
            total = part if total is None else total + part
            dq = lax.dot_general(ds, keys, (((0,), (0,)), ((), ())),
                                 preferred_element_type=jnp.float32) * SCALE
            for g in range(CHUNK):
                dq_ref[first:first + LB, (at + g) * HEAD_SIZE:(at + g + 1) * HEAD_SIZE] = (
                    dq[g * LB:(g + 1) * LB])
        out[...] = (total * SCALE).astype(out.dtype).reshape(out.shape)


WIDE = GROUP * HEAD_SIZE
WIDTH = KEY_VALUE_HEADS * HEAD_SIZE
TOK = LB + SB


def block(rows, columns):
    return pl.BlockSpec((rows, columns), lambda k, *_: (0, k))


def long_block(at):
    return pl.BlockSpec((N_CTX, LB, HEAD_SIZE), lambda k, *_: (0, at, k))


def scratch():
    return [pltpu.VMEM((N_CTX * LB, LANES), jnp.float32), pltpu.VMEM((SB, LANES), jnp.float32)]


LONG_ROWS = jax.ShapeDtypeStruct((N_CTX, LB, WIDTH), jnp.bfloat16)


def dvalues(scalars, queries, upstream, keys, all_keys):
    return pl.pallas_call(
        dvalue_kernel,
        grid_spec=pltpu.PrefetchScalarGridSpec(
            num_scalar_prefetch=3,
            grid=(KEY_VALUE_HEADS,),
            in_specs=[block(TOK, WIDE), block(TOK, WIDE), block(TOK, HEAD_SIZE), long_block(0)],
            out_specs=[long_block(0), block(SB, HEAD_SIZE)],
            scratch_shapes=scratch(),
        ),
        out_shape=[LONG_ROWS, jax.ShapeDtypeStruct((SB, WIDTH), jnp.bfloat16)],
        compiler_params=pltpu.CompilerParams(vmem_limit_bytes=32 << 20),
        cost_estimate=pl.CostEstimate(flops=700_000_000, bytes_accessed=4 << 20, transcendentals=1 << 20),
    )(*scalars, queries, upstream, keys, all_keys)


def dscores(scalars, queries, upstream, keys, values, all_keys, spread_rows):
    return pl.pallas_call(
        dscore_kernel,
        grid_spec=pltpu.PrefetchScalarGridSpec(
            num_scalar_prefetch=3,
            grid=(KEY_VALUE_HEADS,),
            in_specs=[block(TOK, WIDE), block(TOK, WIDE), block(TOK, HEAD_SIZE), block(TOK, HEAD_SIZE),
                      long_block(0), long_block(TOK // LB)],
            out_specs=[block(TOK, WIDE), long_block(0), block(SB, HEAD_SIZE)],
            scratch_shapes=scratch(),
        ),
        out_shape=[jax.ShapeDtypeStruct((TOK, QUERY_HEADS * HEAD_SIZE), jnp.float32), LONG_ROWS,
                   jax.ShapeDtypeStruct((SB, WIDTH), jnp.float32)],
        compiler_params=pltpu.CompilerParams(vmem_limit_bytes=32 << 20),
        cost_estimate=pl.CostEstimate(flops=1_400_000_000, bytes_accessed=6 << 20, transcendentals=1 << 20),
    )(*scalars, queries, upstream, keys, values, all_keys, spread_rows)


Y_LO, CORES = 2, 2
DP = ("ylo", "z", "core")
CTX = ("yhi", "x")


PIECE = 32
DP_BLOCK = N_CTX * PIECE
TOGETHER = 4


def whole(count=1):
    return [pl.BlockSpec(memory_space=pltpu.VMEM)] * count


def regroup_kernel(me_ref, *refs):
    *block_refs, out_ref = refs
    for member in range(N_CTX):
        out_ref[member] = jnp.concatenate(
            [ref[:, member * PIECE:(member + 1) * PIECE] for ref in block_refs], axis=1)


def regroup(me, tokens):
    rows, width = tokens.shape
    depth = width // (DP_BLOCK * Y_LO * CORES)

    def source(at):
        def index(g, me_ref):
            slot = g * TOGETHER + at
            core, y_lo, z = slot // (Y_LO * depth), slot // depth % Y_LO, slot % depth
            return 0, ((y_lo * depth + z) * CORES + core) ^ me_ref[0]
        return pl.BlockSpec((rows, DP_BLOCK), index)

    return pl.pallas_call(
        regroup_kernel,
        grid_spec=pltpu.PrefetchScalarGridSpec(
            num_scalar_prefetch=1,
            grid=(width // (DP_BLOCK * TOGETHER),),
            in_specs=[source(at) for at in range(TOGETHER)],
            out_specs=pl.BlockSpec((N_CTX, rows, PIECE * TOGETHER), lambda g, *_: (0, 0, g)),
        ),
        out_shape=jax.ShapeDtypeStruct((N_CTX, rows, width // N_CTX), tokens.dtype),
        cost_estimate=pl.CostEstimate(flops=0, bytes_accessed=4 << 20, transcendentals=0),
    )(me[None], *[tokens] * TOGETHER)


def values_kernel(tokens_ref, mine_ref, theirs_ref, dv_ref, out_ref):
    weight = jnp.concatenate([mine_ref[...], theirs_ref[...]], axis=0)
    for member in range(0, N_CTX, 2):
        part = jnp.dot(tokens_ref[member * TOK:(member + 2) * TOK], weight,
                       preferred_element_type=jnp.float32).astype(out_ref.dtype)
        out_ref[member, LB:] = part[:TOK]
        out_ref[member + 1, LB:] = part[TOK:]
    out_ref[:, :LB] = dv_ref[...]


def value_parts(tokens, mine, theirs, dv_all):
    return pl.pallas_call(
        values_kernel,
        in_specs=whole(4),
        out_specs=whole()[0],
        out_shape=jax.ShapeDtypeStruct((N_CTX, LB + TOK, WIDTH), jnp.bfloat16),
        compiler_params=pltpu.CompilerParams(vmem_limit_bytes=32 << 20),
        cost_estimate=pl.CostEstimate(flops=2 * tokens.size * WIDTH, bytes_accessed=6 << 20,
                                      transcendentals=0),
    )(tokens, mine, theirs, dv_all)


def added_up(ref, first, last):
    total = ref[0, first:last].astype(jnp.float32)
    for piece in range(1, ref.shape[0]):
        total += ref[piece, first:last].astype(jnp.float32)
    return total


def middle_kernel(parts_ref, dv_short_ref, out_ref, values_ref):
    values_ref[...] = added_up(parts_ref, LB, LB + TOK).astype(values_ref.dtype)
    dv_long = added_up(parts_ref, 0, LB).astype(out_ref.dtype)
    for member in range(N_CTX):
        out_ref[member, :LB] = dv_long
        out_ref[member, LB:TOK] = dv_short_ref[...]
        out_ref[member, TOK:] = values_ref[:LB]


def middle(parts, dv_short):
    return pl.pallas_call(
        middle_kernel,
        in_specs=whole(2),
        out_specs=whole(2),
        out_shape=[jax.ShapeDtypeStruct(parts.shape, parts.dtype),
                   jax.ShapeDtypeStruct((TOK, WIDTH), jnp.bfloat16)],
        cost_estimate=pl.CostEstimate(flops=parts.size, bytes_accessed=4 * parts.size, transcendentals=0),
    )(parts, dv_short)


def closing_kernel(pieces_ref, dk_ref, out_ref):
    share = added_up(pieces_ref, 0, PIECE).astype(out_ref.dtype)
    for member in range(N_CTX):
        out_ref[member, :PIECE] = share
    out_ref[:, PIECE:] = dk_ref[...]


def closing(pieces, dk_all):
    return pl.pallas_call(
        closing_kernel,
        in_specs=whole(2),
        out_specs=whole()[0],
        out_shape=jax.ShapeDtypeStruct((N_CTX, PIECE + LB, WIDTH), jnp.bfloat16),
        cost_estimate=pl.CostEstimate(flops=pieces.size, bytes_accessed=4 * pieces.size, transcendentals=0),
    )(pieces, dk_all)


def last_kernel(parts_ref, dk_short_ref, dk_ref, grad_ref):
    dk_ref[:LB] = added_up(parts_ref, PIECE, PIECE + LB)
    dk_ref[LB:] = dk_short_ref[...]
    grad_ref[...] = parts_ref[:, :PIECE].astype(grad_ref.dtype).reshape(grad_ref.shape)


def last(parts, dk_short):
    return pl.pallas_call(
        last_kernel,
        in_specs=whole(2),
        out_specs=whole(2),
        out_shape=[jax.ShapeDtypeStruct((TOK, WIDTH), jnp.float32),
                   jax.ShapeDtypeStruct((DP_BLOCK, WIDTH), jnp.float32)],
        cost_estimate=pl.CostEstimate(flops=parts.size, bytes_accessed=4 * parts.size, transcendentals=0),
    )(parts, dk_short)


def weight_kernel(half, me_ref, tokens_ref, d_value_ref, *refs):
    *add_refs, out_ref = refs
    count, rows, columns = out_ref.shape
    some = min(DP_BLOCK // PIECE, count)
    d_value = d_value_ref[:, :TOK].reshape(N_CTX * TOK, columns)
    for first in range(0, count, some):
        at = (half * count + first) * rows
        part = lax.dot_general(
            tokens_ref[:, at:at + some * rows], d_value, (((0,), (0,)), ((), ())),
            preferred_element_type=jnp.float32)
        for slot in range(some):
            block = (first + slot) ^ me_ref[0]
            piece = part[slot * rows:(slot + 1) * rows]
            for ref in add_refs:
                piece += ref[block].astype(jnp.float32)
            out_ref[block] = piece.astype(out_ref.dtype)


def weight_share(half, me, tokens, d_value, *added):
    count, columns = tokens.shape[1] // (CORES * PIECE), WIDTH
    return pl.pallas_call(
        functools.partial(weight_kernel, half),
        in_specs=[pl.BlockSpec(memory_space=pltpu.SMEM)] + whole(2 + len(added)),
        out_specs=whole()[0],
        out_shape=jax.ShapeDtypeStruct((count, PIECE, columns), jnp.bfloat16),
        compiler_params=pltpu.CompilerParams(vmem_limit_bytes=32 << 20),
        cost_estimate=pl.CostEstimate(flops=tokens.size * columns, bytes_accessed=3 << 20,
                                      transcendentals=0),
    )(me[None], tokens, d_value, *added)


def exchange(pieces, axes):
    return lax.all_to_all(pieces, axes, 0, 0, tiled=True)


def spread(piece, axes):
    count = lax.axis_size(axes)
    return exchange(jnp.broadcast_to(piece[None], (count,) + piece.shape), axes)


def swap_along(array, axis, step):
    count = lax.axis_size(axis)
    return lax.ppermute(array, axis, [(i, i ^ step) for i in range(count)])


def after(value, other):
    return lax.optimization_barrier((value, other))[0]


def on_device(tokens, queries, rotated_key_rows, upstream, value_projection_weight, doc_lengths,
              stretch_order):
    member = lax.axis_index(CTX)
    plane = lax.axis_index(("ylo", "z"))
    order = stretch_order[0]
    scalars = (order, lax.dynamic_slice(order, (member,), (1,)), jnp.cumsum(doc_lengths[0]))

    all_keys = spread(rotated_key_rows[:LB], CTX)
    grouped = regroup(plane * CORES + lax.axis_index("core"), tokens)
    grouped, all_keys = lax.optimization_barrier((grouped, all_keys))
    tok = exchange(grouped, CTX).reshape(N_CTX * TOK, -1)
    dv_all, dv_short = dvalues(scalars, queries, upstream, rotated_key_rows, all_keys)

    weight = lax.dynamic_slice_in_dim(value_projection_weight, member * PIECE, PIECE, 0)
    weight = after(weight, grouped)
    step = 1
    while step < lax.axis_size("z"):
        if step == 4:
            weight = after(weight, dv_all)
        weight = jnp.concatenate([weight, swap_along(weight, "z", step)], axis=0)
        step *= 2
    weight = jnp.concatenate([weight, swap_along(weight, "ylo", 1)], axis=0)
    other_weight = swap_along(weight, "core", 1)

    parts = exchange(value_parts(tok, weight, other_weight, dv_all), CTX)
    spread_rows, values = middle(parts, dv_short)
    spread_rows = exchange(spread_rows, CTX)

    share = swap_along(weight_share(1, plane, tok, spread_rows), "core", 1)
    share = weight_share(0, plane, tok, spread_rows, share)
    values = after(values, share)
    share = exchange(share, ("ylo", "z"))
    d_query, dk_all, dk_short = dscores(scalars, queries, upstream, rotated_key_rows, values,
                                        all_keys, spread_rows)
    d_key, weight_grad = last(exchange(closing(share, dk_all), CTX), dk_short)
    return d_query, d_key, weight_grad


def solution(mesh):
    packs = mesh.shape["dp"]
    mesh = Mesh(mesh.devices.reshape(Y_LO, packs // (Y_LO * CORES), CORES, 2, N_CTX // 2), DP + CTX)
    rows = P(DP + CTX, None)
    return jax.shard_map(
        on_device,
        mesh=mesh,
        in_specs=(rows, rows, rows, rows, P(DP, None), rows, P(DP, None)),
        out_specs=(rows, rows, P(DP, None)),
        check_vma=False,
    )
```

```python
import functools
import math

import jax
import jax.numpy as jnp
from jax import lax
from jax.experimental import pallas as pl
from jax.experimental.pallas import tpu as pltpu
from jax.sharding import Mesh
from jax.sharding import PartitionSpec as P

QUERY_HEADS = 32
KEY_VALUE_HEADS = 4
HEAD_SIZE = 128
GROUP = QUERY_HEADS // KEY_VALUE_HEADS
LB = 64
SB = 64
S_DOCS = 4
N_CTX = 8
CHUNK = 4
LANES = CHUNK * LB
SCALE = HEAD_SIZE ** -0.5
NEG = -1e30


def fill_masks(order_ref, place_ref, ends_ref, long_bias, short_bias):
    key = lax.broadcasted_iota(jnp.int32, (LB, LANES), 0)
    query = lax.broadcasted_iota(jnp.int32, (LB, LANES), 1) & (LB - 1)
    mine = place_ref[0]
    for block in range(N_CTX):
        ahead = order_ref[block] * LB + key <= mine * LB + query
        long_bias[pl.ds(block * LB, LB), :] = jnp.where(ahead, 0.0, NEG)
    fill_short_mask(ends_ref, short_bias)


def fill_short_mask(ends_ref, short_bias):
    key = lax.broadcasted_iota(jnp.int32, (SB, LANES), 0)
    query = lax.broadcasted_iota(jnp.int32, (SB, LANES), 1) & (LB - 1)
    key_doc = jnp.zeros((SB, LANES), jnp.int32)
    query_doc = jnp.zeros((SB, LANES), jnp.int32)
    for doc in range(S_DOCS):
        key_doc += (key >= ends_ref[doc]).astype(jnp.int32)
        query_doc += (query >= ends_ref[doc]).astype(jnp.int32)
    short_bias[...] = jnp.where((key_doc == query_doc) & (key <= query), 0.0, NEG)


def head_rows(ref, first, at):
    return jnp.concatenate(
        [ref[first:first + LB, (at + g) * HEAD_SIZE:(at + g + 1) * HEAD_SIZE] for g in range(CHUNK)],
        axis=0,
    )


def probs(keys, q_rows, bias):
    s = lax.dot_general(keys, q_rows, (((1,), (1,)), ((), ())), preferred_element_type=jnp.float32)
    s = s * (SCALE * math.log2(math.e)) + bias
    e = jnp.exp2(s - jnp.max(s, axis=0, keepdims=True))
    return e * (1.0 / jnp.sum(e, axis=0, keepdims=True))


def fetch(sources, buffers, sems):
    def copy(at, head):
        source, rows, lanes = sources[at]
        return pltpu.make_async_copy(
            source.at[rows + (pl.ds(pl.multiple_of(head * lanes, lanes), lanes),)],
            buffers[at].at[head], sems.at[at, head])

    step = pl.program_id(0)

    @pl.when(step == 0)
    def _():
        for head in range(KEY_VALUE_HEADS):
            for at in range(len(sources)):
                copy(at, head).start()

    for at in range(len(sources)):
        copy(at, step).wait()
    return [buffer.at[step] for buffer in buffers]


ALL = slice(None)


def short_dvalue_kernel(ends_ref, q_ref, u_ref, ks_ref, out_ref, short_bias):
    @pl.when(pl.program_id(0) == 0)
    def _():
        fill_short_mask(ends_ref, short_bias)

    total = None
    for at in range(0, GROUP, CHUNK):
        p = probs(ks_ref[...], head_rows(q_ref, 0, at), short_bias[...]).astype(jnp.bfloat16)
        part = jnp.dot(p, head_rows(u_ref, 0, at), preferred_element_type=jnp.float32)
        total = part if total is None else total + part
    out_ref[...] = total.astype(out_ref.dtype)


def dvalue_kernel(order_ref, place_ref, ends_ref, q_hbm, u_hbm, k_ref, dvl_ref,
                  long_bias, short_bias, q_buffer, u_buffer, sems):
    rows = (pl.ds(0, LB),)
    q_ref, u_ref = fetch([(q_hbm, rows, WIDE), (u_hbm, rows, WIDE)], [q_buffer, u_buffer], sems)

    @pl.when(pl.program_id(0) == 0)
    def _():
        fill_masks(order_ref, place_ref, ends_ref, long_bias, short_bias)

    keys = k_ref[...].reshape(N_CTX * LB, HEAD_SIZE)
    total = None
    for at in range(0, GROUP, CHUNK):
        p = probs(keys, head_rows(q_ref, 0, at), long_bias[...]).astype(jnp.bfloat16)
        part = jnp.dot(p, head_rows(u_ref, 0, at), preferred_element_type=jnp.float32)
        total = part if total is None else total + part
    dvl_ref[...] = total.astype(dvl_ref.dtype).reshape(dvl_ref.shape)


def dscore_kernel(order_ref, place_ref, ends_ref, q_hbm, u_hbm, ks_ref, vs_ref, k_ref, v_hbm,
                  dq_ref, dkl_ref, dks_ref, long_bias, short_bias, q_buffer, u_buffer, v_buffer, sems):
    q_ref, u_ref, v_ref = fetch(
        [(q_hbm, (ALL,), WIDE), (u_hbm, (ALL,), WIDE), (v_hbm, (ALL, pl.ds(LB, LB)), HEAD_SIZE)],
        [q_buffer, u_buffer, v_buffer], sems)

    @pl.when(pl.program_id(0) == 0)
    def _():
        fill_masks(order_ref, place_ref, ends_ref, long_bias, short_bias)

    long_shape = (N_CTX * LB, HEAD_SIZE)
    for first, keys, values, bias, out in (
        (0, k_ref[...].reshape(long_shape), v_ref[...].reshape(long_shape), long_bias, dkl_ref),
        (LB, ks_ref[LB:, :], vs_ref[LB:, :], short_bias, dks_ref),
    ):
        total = None
        for at in range(0, GROUP, CHUNK):
            q_rows = head_rows(q_ref, first, at)
            p = probs(keys, q_rows, bias[...])
            dp = lax.dot_general(values, head_rows(u_ref, first, at), (((1,), (1,)), ((), ())),
                                 preferred_element_type=jnp.float32)
            delta = jnp.sum(p * dp, axis=0, keepdims=True)
            ds = (p * (dp - delta)).astype(jnp.bfloat16)
            part = jnp.dot(ds, q_rows, preferred_element_type=jnp.float32)
            total = part if total is None else total + part
            dq = lax.dot_general(ds, keys, (((0,), (0,)), ((), ())),
                                 preferred_element_type=jnp.float32) * SCALE
            for g in range(CHUNK):
                dq_ref[first:first + LB, (at + g) * HEAD_SIZE:(at + g + 1) * HEAD_SIZE] = (
                    dq[g * LB:(g + 1) * LB])
        out[...] = (total * SCALE).astype(out.dtype).reshape(out.shape)


WIDE = GROUP * HEAD_SIZE
WIDTH = KEY_VALUE_HEADS * HEAD_SIZE
TOK = LB + SB
SHORT_ROWS = KEY_VALUE_HEADS * SB


def block(rows, columns):
    return pl.BlockSpec((rows, columns), lambda k, *_: (0, k))


def long_block(at):
    return pl.BlockSpec((N_CTX, LB, HEAD_SIZE), lambda k, *_: (0, at, k))


def scratch(*fetched):
    return [pltpu.VMEM((N_CTX * LB, LANES), jnp.float32), pltpu.VMEM((SB, LANES), jnp.float32)] + [
        pltpu.VMEM((KEY_VALUE_HEADS,) + shape, jnp.bfloat16) for shape in fetched
    ] + [pltpu.SemaphoreType.DMA((len(fetched), KEY_VALUE_HEADS))]


ELSEWHERE = pl.BlockSpec(memory_space=pltpu.HBM)


LONG_ROWS = jax.ShapeDtypeStruct((N_CTX, LB, WIDTH), jnp.bfloat16)


def short_dvalues(ends, queries, upstream, keys):
    def rows(columns):
        return pl.BlockSpec((SB, columns), lambda k, *_: (1, k))

    return pl.pallas_call(
        short_dvalue_kernel,
        grid_spec=pltpu.PrefetchScalarGridSpec(
            num_scalar_prefetch=1,
            grid=(KEY_VALUE_HEADS,),
            in_specs=[rows(WIDE), rows(WIDE), rows(HEAD_SIZE)],
            out_specs=pl.BlockSpec((SB, HEAD_SIZE), lambda k, *_: (k, 0)),
            scratch_shapes=[pltpu.VMEM((SB, LANES), jnp.float32)],
        ),
        out_shape=jax.ShapeDtypeStruct((SHORT_ROWS, HEAD_SIZE), jnp.bfloat16),
        compiler_params=pltpu.CompilerParams(vmem_limit_bytes=16 << 20),
        cost_estimate=pl.CostEstimate(flops=70_000_000, bytes_accessed=1 << 20, transcendentals=1 << 17),
    )(ends, queries, upstream, keys)


def dvalues(scalars, queries, upstream, all_keys):
    return pl.pallas_call(
        dvalue_kernel,
        grid_spec=pltpu.PrefetchScalarGridSpec(
            num_scalar_prefetch=3,
            grid=(KEY_VALUE_HEADS,),
            in_specs=[ELSEWHERE, ELSEWHERE, long_block(0)],
            out_specs=long_block(0),
            scratch_shapes=scratch((LB, WIDE), (LB, WIDE)),
        ),
        out_shape=LONG_ROWS,
        compiler_params=pltpu.CompilerParams(vmem_limit_bytes=16 << 20),
        cost_estimate=pl.CostEstimate(flops=600_000_000, bytes_accessed=4 << 20, transcendentals=1 << 20),
    )(*scalars, queries, upstream, all_keys)


def dscores(scalars, queries, upstream, keys, values, all_keys, spread_rows):
    return pl.pallas_call(
        dscore_kernel,
        grid_spec=pltpu.PrefetchScalarGridSpec(
            num_scalar_prefetch=3,
            grid=(KEY_VALUE_HEADS,),
            in_specs=[ELSEWHERE, ELSEWHERE, block(TOK, HEAD_SIZE), block(TOK, HEAD_SIZE),
                      long_block(0), ELSEWHERE],
            out_specs=[block(TOK, WIDE), long_block(0), block(SB, HEAD_SIZE)],
            scratch_shapes=scratch((TOK, WIDE), (TOK, WIDE), (N_CTX, LB, HEAD_SIZE)),
        ),
        out_shape=[jax.ShapeDtypeStruct((TOK, QUERY_HEADS * HEAD_SIZE), jnp.float32), LONG_ROWS,
                   jax.ShapeDtypeStruct((SB, WIDTH), jnp.float32)],
        compiler_params=pltpu.CompilerParams(vmem_limit_bytes=60 << 20),
        cost_estimate=pl.CostEstimate(flops=1_400_000_000, bytes_accessed=6 << 20, transcendentals=1 << 20),
    )(*scalars, queries, upstream, keys, values, all_keys, spread_rows)


Y_LO, CORES = 2, 2
DP = ("ylo", "z", "core")
CTX = ("yhi", "x")


PIECE = 32
DP_BLOCK = N_CTX * PIECE
TOGETHER = 4


def whole(count=1):
    return [pl.BlockSpec(memory_space=pltpu.VMEM)] * count


def regroup_kernel(me_ref, *refs):
    *block_refs, short_ref, out_ref = refs
    rows = block_refs[0].shape[0]
    for member in range(N_CTX):
        out_ref[member, rows:] = short_ref[...]
        out_ref[member, :rows] = jnp.concatenate(
            [ref[:, member * PIECE:(member + 1) * PIECE] for ref in block_refs], axis=1)


def turned(slot, depth):
    z, bits = 0, depth.bit_length() - 1
    for bit in range(bits):
        z = z + ((slot >> bit) & 1) * (1 << (bits - 1 - bit))
    return z


def short_rows(ref, member, head):
    step = SHORT_ROWS // (ref.shape[2] // HEAD_SIZE)
    if step >= SB:
        g, at = divmod(head * SB, step)
        return ref[member, TOK + at:TOK + at + SB, g * HEAD_SIZE:(g + 1) * HEAD_SIZE]
    return jnp.concatenate(
        [ref[member, TOK:TOK + step, g * HEAD_SIZE:(g + 1) * HEAD_SIZE]
         for g in range(head * SB // step, (head + 1) * SB // step)], axis=0)


def regroup(me, tokens, dv_short):
    rows, width = tokens.shape
    depth = width // (DP_BLOCK * Y_LO * CORES)
    steps = width // (DP_BLOCK * TOGETHER)
    extra = SHORT_ROWS // steps

    def source(at):
        def index(g, me_ref):
            slot = g * TOGETHER + at
            core, y_lo, z = slot // (Y_LO * depth), slot // depth % Y_LO, turned(slot % depth, depth)
            return 0, ((y_lo * depth + z) * CORES + core) ^ me_ref[0]
        return pl.BlockSpec((rows, DP_BLOCK), index)

    return pl.pallas_call(
        regroup_kernel,
        grid_spec=pltpu.PrefetchScalarGridSpec(
            num_scalar_prefetch=1,
            grid=(steps,),
            in_specs=[source(at) for at in range(TOGETHER)]
            + [pl.BlockSpec((extra, HEAD_SIZE), lambda g, *_: (g, 0))],
            out_specs=pl.BlockSpec((N_CTX, rows + extra, PIECE * TOGETHER), lambda g, *_: (0, 0, g)),
        ),
        out_shape=jax.ShapeDtypeStruct((N_CTX, rows + extra, width // N_CTX), tokens.dtype),
        cost_estimate=pl.CostEstimate(flops=0, bytes_accessed=4 << 20, transcendentals=0),
    )(me[None], *[tokens] * TOGETHER, dv_short)


def values_kernel(tokens_ref, mine_ref, theirs_ref, dv_ref, out_ref):
    weight = jnp.concatenate([mine_ref[...], theirs_ref[...]], axis=0)
    for member in range(0, N_CTX, 2):
        both = jnp.concatenate([tokens_ref[member, :TOK], tokens_ref[member + 1, :TOK]], axis=0)
        part = jnp.dot(both, weight, preferred_element_type=jnp.float32).astype(out_ref.dtype)
        out_ref[member, LB:] = part[:TOK]
        out_ref[member + 1, LB:] = part[TOK:]
    out_ref[:, :LB] = dv_ref[...]


def value_parts(tokens, mine, theirs, dv_all):
    return pl.pallas_call(
        values_kernel,
        in_specs=whole(4),
        out_specs=whole()[0],
        out_shape=jax.ShapeDtypeStruct((N_CTX, LB + TOK, WIDTH), jnp.bfloat16),
        compiler_params=pltpu.CompilerParams(vmem_limit_bytes=16 << 20),
        cost_estimate=pl.CostEstimate(flops=2 * tokens.size * WIDTH, bytes_accessed=6 << 20,
                                      transcendentals=0),
    )(tokens, mine, theirs, dv_all)


def added_up(ref, first, last):
    total = ref[0, first:last].astype(jnp.float32)
    for piece in range(1, ref.shape[0]):
        total += ref[piece, first:last].astype(jnp.float32)
    return total


def middle_kernel(parts_ref, out_ref, values_ref):
    values_ref[...] = added_up(parts_ref, LB, LB + TOK).astype(values_ref.dtype)
    dv_long = added_up(parts_ref, 0, LB).astype(out_ref.dtype)
    for member in range(N_CTX):
        out_ref[member, :LB] = dv_long
        out_ref[member, LB:] = values_ref[:LB]


def middle(parts):
    return pl.pallas_call(
        middle_kernel,
        in_specs=whole(1),
        out_specs=whole(2),
        out_shape=[jax.ShapeDtypeStruct((N_CTX, 2 * LB, WIDTH), parts.dtype),
                   jax.ShapeDtypeStruct((TOK, WIDTH), jnp.bfloat16)],
        cost_estimate=pl.CostEstimate(flops=parts.size, bytes_accessed=4 * parts.size, transcendentals=0),
    )(parts)


def closing_kernel(pieces_ref, dk_ref, out_ref):
    share = added_up(pieces_ref, 0, PIECE).astype(out_ref.dtype)
    for member in range(N_CTX):
        out_ref[member, :PIECE] = share
    out_ref[:, PIECE:] = dk_ref[...]


def closing(pieces, dk_all):
    return pl.pallas_call(
        closing_kernel,
        in_specs=whole(2),
        out_specs=whole()[0],
        out_shape=jax.ShapeDtypeStruct((N_CTX, PIECE + LB, WIDTH), jnp.bfloat16),
        cost_estimate=pl.CostEstimate(flops=pieces.size, bytes_accessed=4 * pieces.size, transcendentals=0),
    )(pieces, dk_all)


def last_kernel(parts_ref, dk_short_ref, dk_ref, grad_ref):
    dk_ref[:LB] = added_up(parts_ref, PIECE, PIECE + LB)
    dk_ref[LB:] = dk_short_ref[...]
    grad_ref[...] = parts_ref[:, :PIECE].astype(grad_ref.dtype).reshape(grad_ref.shape)


def last(parts, dk_short):
    return pl.pallas_call(
        last_kernel,
        in_specs=whole(2),
        out_specs=whole(2),
        out_shape=[jax.ShapeDtypeStruct((TOK, WIDTH), jnp.float32),
                   jax.ShapeDtypeStruct((DP_BLOCK, WIDTH), jnp.float32)],
        cost_estimate=pl.CostEstimate(flops=parts.size, bytes_accessed=4 * parts.size, transcendentals=0),
    )(parts, dk_short)


def weight_kernel(half, me_ref, tokens_ref, d_value_ref, *refs):
    *add_refs, out_ref = refs
    count, rows, columns = out_ref.shape
    some = min(DP_BLOCK // PIECE, count)
    d_value = jnp.concatenate(
        [rows for member in range(N_CTX) for rows in (
            d_value_ref[member, :LB],
            jnp.concatenate([short_rows(tokens_ref, member, head) for head in range(KEY_VALUE_HEADS)], axis=1),
        )], axis=0)
    for first in range(0, count, some):
        at = (half * count + first) * rows
        part = lax.dot_general(
            tokens_ref[:, :TOK, at:at + some * rows].reshape(N_CTX * TOK, some * rows), d_value, (((0,), (0,)), ((), ())),
            preferred_element_type=jnp.float32)
        for slot in range(some):
            depth = count // Y_LO
            y_lo, z = divmod(first + slot, depth)
            block = (y_lo * depth + turned(z, depth)) ^ me_ref[0]
            piece = part[slot * rows:(slot + 1) * rows]
            for ref in add_refs:
                piece += ref[block].astype(jnp.float32)
            out_ref[block] = piece.astype(out_ref.dtype)


def weight_share(half, me, tokens, d_value, *added):
    count, columns = tokens.shape[2] // (CORES * PIECE), WIDTH
    return pl.pallas_call(
        functools.partial(weight_kernel, half),
        in_specs=[pl.BlockSpec(memory_space=pltpu.SMEM)] + whole(2 + len(added)),
        out_specs=whole()[0],
        out_shape=jax.ShapeDtypeStruct((count, PIECE, columns), jnp.bfloat16),
        compiler_params=pltpu.CompilerParams(vmem_limit_bytes=16 << 20),
        cost_estimate=pl.CostEstimate(flops=tokens.size * columns, bytes_accessed=3 << 20,
                                      transcendentals=0),
    )(me[None], tokens, d_value, *added)


def exchange(pieces, axes):
    return lax.all_to_all(pieces, axes, 0, 0, tiled=True)


def spread(piece, axes):
    count = lax.axis_size(axes)
    return exchange(jnp.broadcast_to(piece[None], (count,) + piece.shape), axes)


def swap_along(array, axis, step):
    count = lax.axis_size(axis)
    return lax.ppermute(array, axis, [(i, i ^ step) for i in range(count)])


def after(value, other):
    return lax.optimization_barrier((value, other))[0]


def on_device(tokens, queries, rotated_key_rows, upstream, value_projection_weight, doc_lengths,
              stretch_order):
    member = lax.axis_index(CTX)
    plane = lax.axis_index(("ylo", "z"))
    order = stretch_order[0]
    scalars = (order, lax.dynamic_slice(order, (member,), (1,)), jnp.cumsum(doc_lengths[0]))

    all_keys = spread(rotated_key_rows[:LB], CTX)
    dv_short = short_dvalues(scalars[2], queries, upstream, rotated_key_rows)
    grouped = regroup(plane * CORES + lax.axis_index("core"), tokens, dv_short)
    grouped, all_keys = lax.optimization_barrier((grouped, all_keys))
    tok = exchange(grouped, CTX)

    weight = lax.dynamic_slice_in_dim(value_projection_weight, member * PIECE, PIECE, 0)
    weight = after(weight, grouped)
    depth = lax.axis_size("z")
    far = [turned(slot, depth) for slot in range(depth // 2)]
    weight = jnp.concatenate([weight] + [swap_along(weight, "z", step) for step in far[1:]], axis=0)
    if depth > 1:
        weight = jnp.concatenate([weight, swap_along(weight, "z", 1)], axis=0)
    dv_all = dvalues(scalars, queries, upstream, after(all_keys, weight))
    weight = jnp.concatenate([weight, swap_along(weight, "ylo", 1)], axis=0)
    other_weight = swap_along(after(weight, dv_all), "core", 1)

    parts = exchange(value_parts(tok, weight, other_weight, dv_all), CTX)
    spread_rows, values = middle(parts)
    spread_rows = exchange(spread_rows, CTX)

    share = swap_along(weight_share(1, plane, tok, spread_rows), "core", 1)
    share = weight_share(0, plane, tok, spread_rows, share)
    values = after(values, share)
    share = exchange(share, ("ylo", "z"))
    d_query, dk_all, dk_short = dscores(scalars, queries, upstream, rotated_key_rows, values,
                                        all_keys, spread_rows)
    d_key, weight_grad = last(exchange(closing(share, dk_all), CTX), dk_short)
    return d_query, d_key, weight_grad


def solution(mesh):
    packs = mesh.shape["dp"]
    mesh = Mesh(mesh.devices.reshape(Y_LO, packs // (Y_LO * CORES), CORES, 2, N_CTX // 2), DP + CTX)
    rows = P(DP + CTX, None)
    return jax.shard_map(
        on_device,
        mesh=mesh,
        in_specs=(rows, rows, rows, rows, P(DP, None), rows, P(DP, None)),
        out_specs=(rows, rows, P(DP, None)),
        check_vma=False,
    )
```

```python
import functools
import math

import jax
import jax.numpy as jnp
from jax import lax
from jax.experimental import pallas as pl
from jax.experimental.pallas import tpu as pltpu
from jax.sharding import Mesh
from jax.sharding import PartitionSpec as P

QUERY_HEADS = 32
KEY_VALUE_HEADS = 4
HEAD_SIZE = 128
GROUP = QUERY_HEADS // KEY_VALUE_HEADS
LB = 64
SB = 64
S_DOCS = 4
N_CTX = 8
CHUNK = 4
LANES = CHUNK * LB
SCALE = HEAD_SIZE ** -0.5
NEG = -1e30


def fill_masks(order_ref, place_ref, ends_ref, long_bias, short_bias):
    key = lax.broadcasted_iota(jnp.int32, (LB, LANES), 0)
    query = lax.broadcasted_iota(jnp.int32, (LB, LANES), 1) & (LB - 1)
    mine = place_ref[0]
    for block in range(N_CTX):
        ahead = order_ref[block] * LB + key <= mine * LB + query
        long_bias[pl.ds(block * LB, LB), :] = jnp.where(ahead, 0.0, NEG)
    key_doc = jnp.zeros((SB, LANES), jnp.int32)
    query_doc = jnp.zeros((SB, LANES), jnp.int32)
    for doc in range(S_DOCS):
        key_doc += (key >= ends_ref[doc]).astype(jnp.int32)
        query_doc += (query >= ends_ref[doc]).astype(jnp.int32)
    short_bias[...] = jnp.where((key_doc == query_doc) & (key <= query), 0.0, NEG)


def head_rows(ref, first, at):
    return jnp.concatenate(
        [ref[first:first + LB, (at + g) * HEAD_SIZE:(at + g + 1) * HEAD_SIZE] for g in range(CHUNK)],
        axis=0,
    )


def probs(keys, q_rows, bias):
    s = lax.dot_general(keys, q_rows, (((1,), (1,)), ((), ())), preferred_element_type=jnp.float32)
    s = s * (SCALE * math.log2(math.e)) + bias
    e = jnp.exp2(s - jnp.max(s, axis=0, keepdims=True))
    return e * (1.0 / jnp.sum(e, axis=0, keepdims=True))


def fetch(sources, buffers, sems):
    def copy(at, head):
        source, rows, lanes = sources[at]
        return pltpu.make_async_copy(
            source.at[rows + (pl.ds(pl.multiple_of(head * lanes, lanes), lanes),)],
            buffers[at].at[head], sems.at[at, head])

    step = pl.program_id(0)

    @pl.when(step == 0)
    def _():
        for head in range(KEY_VALUE_HEADS):
            for at in range(len(sources)):
                copy(at, head).start()

    for at in range(len(sources)):
        copy(at, step).wait()
    return [buffer.at[step] for buffer in buffers]


ALL = slice(None)


def dvalue_kernel(order_ref, place_ref, ends_ref, q_hbm, u_hbm, ks_ref, k_ref,
                  dvl_ref, dvs_ref, long_bias, short_bias, q_buffer, u_buffer, sems):
    q_ref, u_ref = fetch([(q_hbm, (ALL,), WIDE), (u_hbm, (ALL,), WIDE)], [q_buffer, u_buffer], sems)

    @pl.when(pl.program_id(0) == 0)
    def _():
        fill_masks(order_ref, place_ref, ends_ref, long_bias, short_bias)

    for first, keys, bias, out in (
        (0, k_ref[...].reshape(N_CTX * LB, HEAD_SIZE), long_bias, dvl_ref),
        (LB, ks_ref[LB:, :], short_bias, dvs_ref),
    ):
        total = None
        for at in range(0, GROUP, CHUNK):
            p = probs(keys, head_rows(q_ref, first, at), bias[...]).astype(jnp.bfloat16)
            part = jnp.dot(p, head_rows(u_ref, first, at), preferred_element_type=jnp.float32)
            total = part if total is None else total + part
        out[...] = total.astype(out.dtype).reshape(out.shape)


def dscore_kernel(order_ref, place_ref, ends_ref, q_hbm, u_hbm, ks_ref, vs_ref, k_ref, v_hbm,
                  dq_ref, dkl_ref, dks_ref, long_bias, short_bias, q_buffer, u_buffer, v_buffer, sems):
    q_ref, u_ref, v_ref = fetch(
        [(q_hbm, (ALL,), WIDE), (u_hbm, (ALL,), WIDE), (v_hbm, (ALL, pl.ds(TOK, LB)), HEAD_SIZE)],
        [q_buffer, u_buffer, v_buffer], sems)

    @pl.when(pl.program_id(0) == 0)
    def _():
        fill_masks(order_ref, place_ref, ends_ref, long_bias, short_bias)

    long_shape = (N_CTX * LB, HEAD_SIZE)
    for first, keys, values, bias, out in (
        (0, k_ref[...].reshape(long_shape), v_ref[...].reshape(long_shape), long_bias, dkl_ref),
        (LB, ks_ref[LB:, :], vs_ref[LB:, :], short_bias, dks_ref),
    ):
        total = None
        for at in range(0, GROUP, CHUNK):
            q_rows = head_rows(q_ref, first, at)
            p = probs(keys, q_rows, bias[...])
            dp = lax.dot_general(values, head_rows(u_ref, first, at), (((1,), (1,)), ((), ())),
                                 preferred_element_type=jnp.float32)
            delta = jnp.sum(p * dp, axis=0, keepdims=True)
            ds = (p * (dp - delta)).astype(jnp.bfloat16)
            part = jnp.dot(ds, q_rows, preferred_element_type=jnp.float32)
            total = part if total is None else total + part
            dq = lax.dot_general(ds, keys, (((0,), (0,)), ((), ())),
                                 preferred_element_type=jnp.float32) * SCALE
            for g in range(CHUNK):
                dq_ref[first:first + LB, (at + g) * HEAD_SIZE:(at + g + 1) * HEAD_SIZE] = (
                    dq[g * LB:(g + 1) * LB])
        out[...] = (total * SCALE).astype(out.dtype).reshape(out.shape)


WIDE = GROUP * HEAD_SIZE
WIDTH = KEY_VALUE_HEADS * HEAD_SIZE
TOK = LB + SB
PIECE = 32


def block(rows, columns):
    return pl.BlockSpec((rows, columns), lambda k, *_: (0, k))


def long_block(at):
    return pl.BlockSpec((N_CTX, LB, HEAD_SIZE), lambda k, *_: (0, at, k))


def scratch(*more):
    fetched = [(TOK, WIDE), (TOK, WIDE)] + list(more)
    return [pltpu.VMEM((N_CTX * LB, LANES), jnp.float32), pltpu.VMEM((SB, LANES), jnp.float32)] + [
        pltpu.VMEM((KEY_VALUE_HEADS,) + shape, jnp.bfloat16) for shape in fetched
    ] + [pltpu.SemaphoreType.DMA((len(fetched), KEY_VALUE_HEADS))]


ELSEWHERE = pl.BlockSpec(memory_space=pltpu.HBM)


LONG_ROWS = jax.ShapeDtypeStruct((N_CTX, LB, WIDTH), jnp.bfloat16)


def dvalues(scalars, queries, upstream, keys, all_keys):
    return pl.pallas_call(
        dvalue_kernel,
        grid_spec=pltpu.PrefetchScalarGridSpec(
            num_scalar_prefetch=3,
            grid=(KEY_VALUE_HEADS,),
            in_specs=[ELSEWHERE, ELSEWHERE, block(TOK, HEAD_SIZE), long_block(0)],
            out_specs=[long_block(0), block(SB, HEAD_SIZE)],
            scratch_shapes=scratch(),
        ),
        out_shape=[LONG_ROWS, jax.ShapeDtypeStruct((SB, WIDTH), jnp.bfloat16)],
        compiler_params=pltpu.CompilerParams(vmem_limit_bytes=16 << 20),
        cost_estimate=pl.CostEstimate(flops=700_000_000, bytes_accessed=4 << 20, transcendentals=1 << 20),
    )(*scalars, queries, upstream, keys, all_keys)


def dscores(scalars, queries, upstream, keys, values, all_keys, spread_rows):
    return pl.pallas_call(
        dscore_kernel,
        grid_spec=pltpu.PrefetchScalarGridSpec(
            num_scalar_prefetch=3,
            grid=(KEY_VALUE_HEADS,),
            in_specs=[ELSEWHERE, ELSEWHERE, block(TOK, HEAD_SIZE), block(TOK, HEAD_SIZE),
                      long_block(0), ELSEWHERE],
            out_specs=[block(TOK, WIDE), long_block(0), block(SB, HEAD_SIZE)],
            scratch_shapes=scratch((N_CTX, LB, HEAD_SIZE)),
        ),
        out_shape=[jax.ShapeDtypeStruct((TOK, QUERY_HEADS * HEAD_SIZE), jnp.float32), jax.ShapeDtypeStruct((N_CTX, LB + PIECE, WIDTH), jnp.bfloat16),
                   jax.ShapeDtypeStruct((SB, WIDTH), jnp.float32)],
        compiler_params=pltpu.CompilerParams(vmem_limit_bytes=60 << 20),
        cost_estimate=pl.CostEstimate(flops=1_400_000_000, bytes_accessed=6 << 20, transcendentals=1 << 20),
    )(*scalars, queries, upstream, keys, values, all_keys, spread_rows)


Y_LO, CORES = 2, 2
DP = ("ylo", "z", "core")
CTX = ("yhi", "x")


DP_BLOCK = N_CTX * PIECE
TOGETHER = 4


def whole(count=1):
    return [pl.BlockSpec(memory_space=pltpu.VMEM)] * count


def regroup_kernel(me_ref, *refs):
    *block_refs, out_ref = refs
    for member in range(N_CTX):
        out_ref[member] = jnp.concatenate(
            [ref[:, member * PIECE:(member + 1) * PIECE] for ref in block_refs], axis=1)


def turned(slot, depth):
    z, bits = 0, depth.bit_length() - 1
    for bit in range(bits):
        z = z + ((slot >> bit) & 1) * (1 << (bits - 1 - bit))
    return z


def regroup(me, tokens):
    rows, width = tokens.shape
    depth = width // (DP_BLOCK * Y_LO * CORES)

    def source(at):
        def index(g, me_ref):
            slot = g * TOGETHER + at
            core, y_lo, z = slot // (Y_LO * depth), slot % Y_LO, turned(slot // Y_LO % depth, depth)
            return 0, ((y_lo * depth + z) * CORES + core) ^ me_ref[0]
        return pl.BlockSpec((rows, DP_BLOCK), index)

    return pl.pallas_call(
        regroup_kernel,
        grid_spec=pltpu.PrefetchScalarGridSpec(
            num_scalar_prefetch=1,
            grid=(width // (DP_BLOCK * TOGETHER),),
            in_specs=[source(at) for at in range(TOGETHER)],
            out_specs=pl.BlockSpec((N_CTX, rows, PIECE * TOGETHER), lambda g, *_: (0, 0, g)),
        ),
        out_shape=jax.ShapeDtypeStruct((N_CTX, rows, width // N_CTX), tokens.dtype),
        cost_estimate=pl.CostEstimate(flops=0, bytes_accessed=4 << 20, transcendentals=0),
    )(me[None], *[tokens] * TOGETHER)


def values_kernel(tokens_ref, mine_ref, theirs_ref, dv_ref, out_ref):
    weight = jnp.concatenate([mine_ref[...], theirs_ref[...]], axis=0)
    for member in range(0, N_CTX, 2):
        part = jnp.dot(tokens_ref[member * TOK:(member + 2) * TOK], weight,
                       preferred_element_type=jnp.float32).astype(out_ref.dtype)
        out_ref[member, LB:] = part[:TOK]
        out_ref[member + 1, LB:] = part[TOK:]
    out_ref[:, :LB] = dv_ref[...]


def key_copies_kernel(keys_ref, out_ref):
    for member in range(N_CTX):
        out_ref[member] = keys_ref[...]


def key_copies(keys):
    return pl.pallas_call(
        key_copies_kernel,
        grid=(1,),
        in_specs=[pl.BlockSpec((LB, WIDTH), lambda g: (0, 0))],
        out_specs=pl.BlockSpec((N_CTX, LB, WIDTH), lambda g: (0, 0, 0)),
        out_shape=LONG_ROWS,
        cost_estimate=pl.CostEstimate(flops=0, bytes_accessed=1 << 19, transcendentals=0),
    )(keys)


def value_parts(tokens, mine, theirs, dv_all):
    return pl.pallas_call(
        values_kernel,
        in_specs=whole(4),
        out_specs=whole()[0],
        out_shape=jax.ShapeDtypeStruct((N_CTX, LB + TOK, WIDTH), jnp.bfloat16),
        compiler_params=pltpu.CompilerParams(vmem_limit_bytes=16 << 20),
        cost_estimate=pl.CostEstimate(flops=2 * tokens.size * WIDTH, bytes_accessed=6 << 20,
                                      transcendentals=0),
    )(tokens, mine, theirs, dv_all)


def added_up(ref, first, last):
    total = ref[0, first:last].astype(jnp.float32)
    for piece in range(1, ref.shape[0]):
        total += ref[piece, first:last].astype(jnp.float32)
    return total


def middle_kernel(parts_ref, dv_short_ref, out_ref, values_ref):
    values_ref[...] = added_up(parts_ref, LB, LB + TOK).astype(values_ref.dtype)
    dv_long = added_up(parts_ref, 0, LB).astype(out_ref.dtype)
    for member in range(N_CTX):
        out_ref[member, :LB] = dv_long
        out_ref[member, LB:TOK] = dv_short_ref[...]
        out_ref[member, TOK:] = values_ref[:LB]


def middle(parts, dv_short):
    return pl.pallas_call(
        middle_kernel,
        in_specs=whole(2),
        out_specs=whole(2),
        out_shape=[jax.ShapeDtypeStruct(parts.shape, parts.dtype),
                   jax.ShapeDtypeStruct((TOK, WIDTH), jnp.bfloat16)],
        cost_estimate=pl.CostEstimate(flops=parts.size, bytes_accessed=4 * parts.size, transcendentals=0),
    )(parts, dv_short)


def closing_kernel(pieces_ref, _, out_ref):
    share = added_up(pieces_ref, 0, PIECE).astype(out_ref.dtype)
    for member in range(N_CTX):
        out_ref[member] = share


def closing(pieces, payload):
    return pl.pallas_call(
        closing_kernel,
        grid=(1,),
        in_specs=[pl.BlockSpec(pieces.shape, lambda g: (0, 0, 0)), ELSEWHERE],
        out_specs=pl.BlockSpec((N_CTX, PIECE, WIDTH), lambda g: (0, LB // PIECE, 0)),
        out_shape=jax.ShapeDtypeStruct(payload.shape, payload.dtype),
        input_output_aliases={1: 0},
        compiler_params=pltpu.CompilerParams(vmem_limit_bytes=60 << 20),
        cost_estimate=pl.CostEstimate(flops=pieces.size, bytes_accessed=2 * pieces.size, transcendentals=0),
    )(pieces, payload)


def last_kernel(parts_ref, dk_short_ref, dk_ref, grad_ref):
    dk_ref[:LB] = added_up(parts_ref, 0, LB)
    dk_ref[LB:] = dk_short_ref[...]
    grad_ref[...] = parts_ref[:, LB:].astype(grad_ref.dtype).reshape(grad_ref.shape)


def last(parts, dk_short):
    return pl.pallas_call(
        last_kernel,
        in_specs=whole(2),
        out_specs=whole(2),
        out_shape=[jax.ShapeDtypeStruct((TOK, WIDTH), jnp.float32),
                   jax.ShapeDtypeStruct((DP_BLOCK, WIDTH), jnp.float32)],
        cost_estimate=pl.CostEstimate(flops=parts.size, bytes_accessed=4 * parts.size, transcendentals=0),
    )(parts, dk_short)


def weight_kernel(half, me_ref, tokens_ref, d_value_ref, *refs):
    *add_refs, out_ref = refs
    count, rows, columns = out_ref.shape
    some = min(DP_BLOCK // PIECE, count)
    d_value = d_value_ref[:, :TOK].reshape(N_CTX * TOK, columns)
    for first in range(0, count, some):
        at = (half * count + first) * rows
        part = lax.dot_general(
            tokens_ref[:, at:at + some * rows], d_value, (((0,), (0,)), ((), ())),
            preferred_element_type=jnp.float32)
        for slot in range(some):
            depth = count // Y_LO
            z, y_lo = divmod(first + slot, Y_LO)
            block = (y_lo * depth + turned(z, depth)) ^ me_ref[0]
            piece = part[slot * rows:(slot + 1) * rows]
            for ref in add_refs:
                piece += ref[block].astype(jnp.float32)
            out_ref[block] = piece.astype(out_ref.dtype)


def weight_share(half, me, tokens, d_value, *added):
    count, columns = tokens.shape[1] // (CORES * PIECE), WIDTH
    return pl.pallas_call(
        functools.partial(weight_kernel, half),
        in_specs=[pl.BlockSpec(memory_space=pltpu.SMEM)] + whole(2 + len(added)),
        out_specs=whole()[0],
        out_shape=jax.ShapeDtypeStruct((count, PIECE, columns), jnp.bfloat16),
        compiler_params=pltpu.CompilerParams(vmem_limit_bytes=16 << 20),
        cost_estimate=pl.CostEstimate(flops=tokens.size * columns, bytes_accessed=3 << 20,
                                      transcendentals=0),
    )(me[None], tokens, d_value, *added)


def exchange(pieces, axes):
    return lax.all_to_all(pieces, axes, 0, 0, tiled=True)


def swap_along(array, axis, step):
    count = lax.axis_size(axis)
    return lax.ppermute(array, axis, [(i, i ^ step) for i in range(count)])


def after(value, other):
    return lax.optimization_barrier((value, other))[0]


def on_device(tokens, queries, rotated_key_rows, upstream, value_projection_weight, doc_lengths,
              stretch_order):
    member = lax.axis_index(CTX)
    plane = lax.axis_index(("ylo", "z"))
    order = stretch_order[0]
    scalars = (order, lax.dynamic_slice(order, (member,), (1,)), jnp.cumsum(doc_lengths[0]))

    all_keys = exchange(key_copies(rotated_key_rows), CTX)
    grouped = regroup(plane * CORES + lax.axis_index("core"), tokens)
    grouped, all_keys = lax.optimization_barrier((grouped, all_keys))
    tok = exchange(grouped, CTX).reshape(N_CTX * TOK, -1)

    weight = lax.dynamic_slice_in_dim(value_projection_weight, member * PIECE, PIECE, 0)
    weight = after(weight, grouped)
    depth = lax.axis_size("z")
    far = [turned(slot, depth) for slot in range(depth // 2)]
    weight = jnp.concatenate([weight, swap_along(weight, "ylo", 1)], axis=0)
    weight = jnp.concatenate([weight] + [swap_along(weight, "z", step) for step in far[1:]], axis=0)
    dv_all, dv_short = dvalues(scalars, queries, upstream, rotated_key_rows, after(all_keys, weight))
    if depth > 1:
        weight = jnp.concatenate([weight, swap_along(weight, "z", 1)], axis=0)
    other_weight = swap_along(after(weight, dv_all), "core", 1)

    parts = exchange(value_parts(tok, weight, other_weight, dv_all), CTX)
    spread_rows, values = middle(parts, dv_short)
    spread_rows = exchange(spread_rows, CTX)

    share = swap_along(weight_share(1, plane, tok, spread_rows), "core", 1)
    share = weight_share(0, plane, tok, spread_rows, share)
    values = after(values, share)
    share = exchange(share, ("ylo", "z"))
    d_query, dk_all, dk_short = dscores(scalars, queries, upstream, rotated_key_rows, values,
                                        all_keys, spread_rows)
    d_key, weight_grad = last(exchange(closing(share, dk_all), CTX), dk_short)
    return d_query, d_key, weight_grad


def solution(mesh):
    packs = mesh.shape["dp"]
    mesh = Mesh(mesh.devices.reshape(Y_LO, packs // (Y_LO * CORES), CORES, 2, N_CTX // 2), DP + CTX)
    rows = P(DP + CTX, None)
    return jax.shard_map(
        on_device,
        mesh=mesh,
        in_specs=(rows, rows, rows, rows, P(DP, None), rows, P(DP, None)),
        out_specs=(rows, rows, P(DP, None)),
        check_vma=False,
    )
```

```python
import functools
import math

import jax
import jax.numpy as jnp
from jax import lax
from jax.experimental import pallas as pl
from jax.experimental.pallas import tpu as pltpu
from jax.sharding import Mesh
from jax.sharding import PartitionSpec as P

QUERY_HEADS = 32
KEY_VALUE_HEADS = 4
HEAD_SIZE = 128
GROUP = QUERY_HEADS // KEY_VALUE_HEADS
LB = 64
SB = 64
S_DOCS = 4
N_CTX = 8
CHUNK = 4
LANES = CHUNK * LB
SCALE = HEAD_SIZE ** -0.5
NEG = -1e30


def fill_masks(order_ref, place_ref, ends_ref, long_bias, short_bias):
    key = lax.broadcasted_iota(jnp.int32, (LB, LANES), 0)
    query = lax.broadcasted_iota(jnp.int32, (LB, LANES), 1) & (LB - 1)
    mine = place_ref[0]
    for block in range(N_CTX):
        ahead = order_ref[block] * LB + key <= mine * LB + query
        long_bias[pl.ds(block * LB, LB), :] = jnp.where(ahead, 0.0, NEG)
    key_doc = jnp.zeros((SB, LANES), jnp.int32)
    query_doc = jnp.zeros((SB, LANES), jnp.int32)
    for doc in range(S_DOCS):
        key_doc += (key >= ends_ref[doc]).astype(jnp.int32)
        query_doc += (query >= ends_ref[doc]).astype(jnp.int32)
    short_bias[...] = jnp.where((key_doc == query_doc) & (key <= query), 0.0, NEG)


def head_rows(ref, first, at):
    return jnp.concatenate(
        [ref[first:first + LB, (at + g) * HEAD_SIZE:(at + g + 1) * HEAD_SIZE] for g in range(CHUNK)],
        axis=0,
    )


def probs(keys, q_rows, bias):
    s = lax.dot_general(keys, q_rows, (((1,), (1,)), ((), ())), preferred_element_type=jnp.float32)
    s = s * (SCALE * math.log2(math.e)) + bias
    e = jnp.exp2(s - jnp.max(s, axis=0, keepdims=True))
    return e * (1.0 / jnp.sum(e, axis=0, keepdims=True))


def fetch(sources, buffers, sems):
    def copy(at, head):
        source, rows, lanes = sources[at]
        return pltpu.make_async_copy(
            source.at[rows + (pl.ds(pl.multiple_of(head * lanes, lanes), lanes),)],
            buffers[at].at[head], sems.at[at, head])

    step = pl.program_id(0)

    @pl.when(step == 0)
    def _():
        for head in range(KEY_VALUE_HEADS):
            for at in range(len(sources)):
                copy(at, head).start()

    for at in range(len(sources)):
        copy(at, step).wait()
    return [buffer.at[step] for buffer in buffers]


ALL = slice(None)


def dvalue_kernel(order_ref, place_ref, ends_ref, q_hbm, u_hbm, ks_ref, k_ref,
                  dvl_ref, dvs_ref, long_bias, short_bias, q_buffer, u_buffer, sems):
    q_ref, u_ref = fetch([(q_hbm, (ALL,), WIDE), (u_hbm, (ALL,), WIDE)], [q_buffer, u_buffer], sems)

    @pl.when(pl.program_id(0) == 0)
    def _():
        fill_masks(order_ref, place_ref, ends_ref, long_bias, short_bias)

    for first, keys, bias, out in (
        (0, k_ref[...].reshape(N_CTX * LB, HEAD_SIZE), long_bias, dvl_ref),
        (LB, ks_ref[LB:, :], short_bias, dvs_ref),
    ):
        total = None
        for at in range(0, GROUP, CHUNK):
            p = probs(keys, head_rows(q_ref, first, at), bias[...]).astype(jnp.bfloat16)
            part = jnp.dot(p, head_rows(u_ref, first, at), preferred_element_type=jnp.float32)
            total = part if total is None else total + part
        out[...] = total.astype(out.dtype).reshape(out.shape)


def dscore_kernel(order_ref, place_ref, ends_ref, q_hbm, u_hbm, ks_ref, vs_ref, k_ref, v_hbm,
                  dq_ref, dkl_ref, dks_ref, long_bias, short_bias, q_buffer, u_buffer, v_buffer, sems):
    q_ref, u_ref, v_ref = fetch(
        [(q_hbm, (ALL,), WIDE), (u_hbm, (ALL,), WIDE), (v_hbm, (ALL, pl.ds(TOK, LB)), HEAD_SIZE)],
        [q_buffer, u_buffer, v_buffer], sems)

    @pl.when(pl.program_id(0) == 0)
    def _():
        fill_masks(order_ref, place_ref, ends_ref, long_bias, short_bias)

    long_shape = (N_CTX * LB, HEAD_SIZE)
    for first, keys, values, bias, out in (
        (0, k_ref[...].reshape(long_shape), v_ref[...].reshape(long_shape), long_bias, dkl_ref),
        (LB, ks_ref[LB:, :], vs_ref[LB:, :], short_bias, dks_ref),
    ):
        total = None
        for at in range(0, GROUP, CHUNK):
            q_rows = head_rows(q_ref, first, at)
            p = probs(keys, q_rows, bias[...])
            dp = lax.dot_general(values, head_rows(u_ref, first, at), (((1,), (1,)), ((), ())),
                                 preferred_element_type=jnp.float32)
            delta = jnp.sum(p * dp, axis=0, keepdims=True)
            ds = (p * (dp - delta)).astype(jnp.bfloat16)
            part = jnp.dot(ds, q_rows, preferred_element_type=jnp.float32)
            total = part if total is None else total + part
            dq = lax.dot_general(ds, keys, (((0,), (0,)), ((), ())),
                                 preferred_element_type=jnp.float32) * SCALE
            for g in range(CHUNK):
                dq_ref[first:first + LB, (at + g) * HEAD_SIZE:(at + g + 1) * HEAD_SIZE] = (
                    dq[g * LB:(g + 1) * LB])
        out[...] = (total * SCALE).astype(out.dtype).reshape(out.shape)


WIDE = GROUP * HEAD_SIZE
WIDTH = KEY_VALUE_HEADS * HEAD_SIZE
TOK = LB + SB
PIECE = 32


def block(rows, columns):
    return pl.BlockSpec((rows, columns), lambda k, *_: (0, k))


def long_block(at):
    return pl.BlockSpec((N_CTX, LB, HEAD_SIZE), lambda k, *_: (0, at, k))


def scratch(*more):
    fetched = [(TOK, WIDE), (TOK, WIDE)] + list(more)
    return [pltpu.VMEM((N_CTX * LB, LANES), jnp.float32), pltpu.VMEM((SB, LANES), jnp.float32)] + [
        pltpu.VMEM((KEY_VALUE_HEADS,) + shape, jnp.bfloat16) for shape in fetched
    ] + [pltpu.SemaphoreType.DMA((len(fetched), KEY_VALUE_HEADS))]


ELSEWHERE = pl.BlockSpec(memory_space=pltpu.HBM)


LONG_ROWS = jax.ShapeDtypeStruct((N_CTX, LB, WIDTH), jnp.bfloat16)


def dvalues(scalars, queries, upstream, keys, all_keys):
    return pl.pallas_call(
        dvalue_kernel,
        grid_spec=pltpu.PrefetchScalarGridSpec(
            num_scalar_prefetch=3,
            grid=(KEY_VALUE_HEADS,),
            in_specs=[ELSEWHERE, ELSEWHERE, block(TOK, HEAD_SIZE), long_block(0)],
            out_specs=[long_block(0), block(SB, HEAD_SIZE)],
            scratch_shapes=scratch(),
        ),
        out_shape=[LONG_ROWS, jax.ShapeDtypeStruct((SB, WIDTH), jnp.bfloat16)],
        compiler_params=pltpu.CompilerParams(vmem_limit_bytes=16 << 20),
        cost_estimate=pl.CostEstimate(flops=700_000_000, bytes_accessed=4 << 20, transcendentals=1 << 20),
    )(*scalars, queries, upstream, keys, all_keys)


def dscores(scalars, queries, upstream, keys, values, all_keys, spread_rows):
    return pl.pallas_call(
        dscore_kernel,
        grid_spec=pltpu.PrefetchScalarGridSpec(
            num_scalar_prefetch=3,
            grid=(KEY_VALUE_HEADS,),
            in_specs=[ELSEWHERE, ELSEWHERE, block(TOK, HEAD_SIZE), block(TOK, HEAD_SIZE),
                      long_block(0), ELSEWHERE],
            out_specs=[block(TOK, WIDE), long_block(0), block(SB, HEAD_SIZE)],
            scratch_shapes=scratch((N_CTX, LB, HEAD_SIZE)),
        ),
        out_shape=[jax.ShapeDtypeStruct((TOK, QUERY_HEADS * HEAD_SIZE), jnp.float32), jax.ShapeDtypeStruct((N_CTX, LB + PIECE, WIDTH), jnp.bfloat16),
                   jax.ShapeDtypeStruct((SB, WIDTH), jnp.float32)],
        compiler_params=pltpu.CompilerParams(vmem_limit_bytes=60 << 20),
        cost_estimate=pl.CostEstimate(flops=1_400_000_000, bytes_accessed=6 << 20, transcendentals=1 << 20),
    )(*scalars, queries, upstream, keys, values, all_keys, spread_rows)


Y_LO, CORES = 2, 2
DP = ("ylo", "z", "core")
CTX = ("yhi", "x")


DP_BLOCK = N_CTX * PIECE
TOGETHER = 4


def whole(count=1):
    return [pl.BlockSpec(memory_space=pltpu.VMEM)] * count


def regroup_kernel(me_ref, *refs):
    *block_refs, out_ref = refs
    for member in range(N_CTX):
        out_ref[member] = jnp.concatenate(
            [ref[:, member * PIECE:(member + 1) * PIECE] for ref in block_refs], axis=1)


def turned(slot, depth):
    z, bits = 0, depth.bit_length() - 1
    for bit in range(bits):
        z = z + ((slot >> bit) & 1) * (1 << (bits - 1 - bit))
    return z


def regroup(me, tokens):
    rows, width = tokens.shape
    depth = width // (DP_BLOCK * Y_LO * CORES)

    def source(at):
        def index(g, me_ref):
            slot = g * TOGETHER + at
            core, y_lo, z = slot // (Y_LO * depth), slot % Y_LO, turned(slot // Y_LO % depth, depth)
            return 0, ((y_lo * depth + z) * CORES + core) ^ me_ref[0]
        return pl.BlockSpec((rows, DP_BLOCK), index)

    return pl.pallas_call(
        regroup_kernel,
        grid_spec=pltpu.PrefetchScalarGridSpec(
            num_scalar_prefetch=1,
            grid=(width // (DP_BLOCK * TOGETHER),),
            in_specs=[source(at) for at in range(TOGETHER)],
            out_specs=pl.BlockSpec((N_CTX, rows, PIECE * TOGETHER), lambda g, *_: (0, 0, g)),
        ),
        out_shape=jax.ShapeDtypeStruct((N_CTX, rows, width // N_CTX), tokens.dtype),
        cost_estimate=pl.CostEstimate(flops=0, bytes_accessed=4 << 20, transcendentals=0),
    )(me[None], *[tokens] * TOGETHER)


def values_kernel(tokens_ref, mine_ref, theirs_ref, dv_ref, out_ref):
    weight = jnp.concatenate([mine_ref[...], theirs_ref[...]], axis=0)
    for member in range(0, N_CTX, 2):
        part = jnp.dot(tokens_ref[member * TOK:(member + 2) * TOK], weight,
                       preferred_element_type=jnp.float32).astype(out_ref.dtype)
        out_ref[member, LB:] = part[:TOK]
        out_ref[member + 1, LB:] = part[TOK:]
    out_ref[:, :LB] = dv_ref[...]


def key_copies_kernel(keys_ref, out_ref):
    for member in range(N_CTX):
        out_ref[member] = keys_ref[...]


def key_copies(keys):
    return pl.pallas_call(
        key_copies_kernel,
        grid=(1,),
        in_specs=[pl.BlockSpec((LB, WIDTH), lambda g: (0, 0))],
        out_specs=pl.BlockSpec((N_CTX, LB, WIDTH), lambda g: (0, 0, 0)),
        out_shape=LONG_ROWS,
        cost_estimate=pl.CostEstimate(flops=0, bytes_accessed=1 << 19, transcendentals=0),
    )(keys)


def value_parts(tokens, mine, theirs, dv_all):
    return pl.pallas_call(
        values_kernel,
        in_specs=whole(4),
        out_specs=whole()[0],
        out_shape=jax.ShapeDtypeStruct((N_CTX, LB + TOK, WIDTH), jnp.bfloat16),
        compiler_params=pltpu.CompilerParams(vmem_limit_bytes=16 << 20),
        cost_estimate=pl.CostEstimate(flops=2 * tokens.size * WIDTH, bytes_accessed=6 << 20,
                                      transcendentals=0),
    )(tokens, mine, theirs, dv_all)


def added_up(ref, first, last):
    total = ref[0, first:last].astype(jnp.float32)
    for piece in range(1, ref.shape[0]):
        total += ref[piece, first:last].astype(jnp.float32)
    return total


def middle_kernel(parts_ref, dv_short_ref, out_ref, values_ref):
    values_ref[...] = added_up(parts_ref, LB, LB + TOK).astype(values_ref.dtype)
    dv_long = added_up(parts_ref, 0, LB).astype(out_ref.dtype)
    for member in range(N_CTX):
        out_ref[member, :LB] = dv_long
        out_ref[member, LB:TOK] = dv_short_ref[...]
        out_ref[member, TOK:] = values_ref[:LB]


def middle(parts, dv_short):
    return pl.pallas_call(
        middle_kernel,
        in_specs=whole(2),
        out_specs=whole(2),
        out_shape=[jax.ShapeDtypeStruct(parts.shape, parts.dtype),
                   jax.ShapeDtypeStruct((TOK, WIDTH), jnp.bfloat16)],
        cost_estimate=pl.CostEstimate(flops=parts.size, bytes_accessed=4 * parts.size, transcendentals=0),
    )(parts, dv_short)


def closing_kernel(pieces_ref, _, out_ref):
    share = added_up(pieces_ref, 0, PIECE).astype(out_ref.dtype)
    for member in range(N_CTX):
        out_ref[member] = share


def closing(pieces, payload):
    return pl.pallas_call(
        closing_kernel,
        grid=(1,),
        in_specs=[pl.BlockSpec(pieces.shape, lambda g: (0, 0, 0)), ELSEWHERE],
        out_specs=pl.BlockSpec((N_CTX, PIECE, WIDTH), lambda g: (0, LB // PIECE, 0)),
        out_shape=jax.ShapeDtypeStruct(payload.shape, payload.dtype),
        input_output_aliases={1: 0},
        compiler_params=pltpu.CompilerParams(vmem_limit_bytes=60 << 20),
        cost_estimate=pl.CostEstimate(flops=pieces.size, bytes_accessed=2 * pieces.size, transcendentals=0),
    )(pieces, payload)


def last_kernel(parts_ref, dk_short_ref, dk_ref, grad_ref):
    dk_ref[:LB] = added_up(parts_ref, 0, LB)
    dk_ref[LB:] = dk_short_ref[...]
    grad_ref[...] = parts_ref[:, LB:].astype(grad_ref.dtype).reshape(grad_ref.shape)


def last(parts, dk_short):
    return pl.pallas_call(
        last_kernel,
        in_specs=whole(2),
        out_specs=whole(2),
        out_shape=[jax.ShapeDtypeStruct((TOK, WIDTH), jnp.float32),
                   jax.ShapeDtypeStruct((DP_BLOCK, WIDTH), jnp.float32)],
        cost_estimate=pl.CostEstimate(flops=parts.size, bytes_accessed=4 * parts.size, transcendentals=0),
    )(parts, dk_short)


def weight_kernel(half, me_ref, tokens_ref, d_value_ref, *refs):
    *add_refs, out_ref = refs
    count, rows, columns = out_ref.shape
    some = min(DP_BLOCK // PIECE, count)
    d_value = d_value_ref[:, :TOK].reshape(N_CTX * TOK, columns)
    for first in range(0, count, some):
        at = (half * count + first) * rows
        part = lax.dot_general(
            tokens_ref[:, at:at + some * rows], d_value, (((0,), (0,)), ((), ())),
            preferred_element_type=jnp.float32)
        for slot in range(some):
            depth = count // Y_LO
            z, y_lo = divmod(first + slot, Y_LO)
            block = (y_lo * depth + turned(z, depth)) ^ me_ref[0]
            piece = part[slot * rows:(slot + 1) * rows]
            for ref in add_refs:
                piece += ref[block].astype(jnp.float32)
            out_ref[block] = piece.astype(out_ref.dtype)


def weight_share(half, me, tokens, d_value, *added):
    count, columns = tokens.shape[1] // (CORES * PIECE), WIDTH
    return pl.pallas_call(
        functools.partial(weight_kernel, half),
        in_specs=[pl.BlockSpec(memory_space=pltpu.SMEM)] + whole(2 + len(added)),
        out_specs=whole()[0],
        out_shape=jax.ShapeDtypeStruct((count, PIECE, columns), jnp.bfloat16),
        compiler_params=pltpu.CompilerParams(vmem_limit_bytes=16 << 20),
        cost_estimate=pl.CostEstimate(flops=tokens.size * columns, bytes_accessed=3 << 20,
                                      transcendentals=0),
    )(me[None], tokens, d_value, *added)


def exchange(pieces, axes):
    return lax.all_to_all(pieces, axes, 0, 0, tiled=True)


def swap_along(array, axis, step):
    count = lax.axis_size(axis)
    return lax.ppermute(array, axis, [(i, i ^ step) for i in range(count)])


def after(value, other):
    return lax.optimization_barrier((value, other))[0]


def on_device(tokens, queries, rotated_key_rows, upstream, value_projection_weight, doc_lengths,
              stretch_order):
    member = lax.axis_index(CTX)
    plane = lax.axis_index(("ylo", "z"))
    order = stretch_order[0]
    scalars = (order, lax.dynamic_slice(order, (member,), (1,)), jnp.cumsum(doc_lengths[0]))

    all_keys = exchange(key_copies(rotated_key_rows), CTX)
    weight = lax.dynamic_slice_in_dim(value_projection_weight, member * PIECE, PIECE, 0)
    weight = jnp.concatenate([weight, swap_along(weight, "ylo", 1)], axis=0)
    grouped = regroup(after(plane * CORES + lax.axis_index("core"), weight), tokens)
    grouped, all_keys = lax.optimization_barrier((grouped, all_keys))
    tok = exchange(grouped, CTX).reshape(N_CTX * TOK, -1)

    weight = after(weight, grouped)
    depth = lax.axis_size("z")
    far = [turned(slot, depth) for slot in range(depth // 2)]
    weight = jnp.concatenate([weight] + [swap_along(weight, "z", step) for step in far[1:]], axis=0)
    dv_all, dv_short = dvalues(scalars, queries, upstream, rotated_key_rows, after(all_keys, weight))
    if depth > 1:
        weight = jnp.concatenate([weight, swap_along(weight, "z", 1)], axis=0)
    other_weight = swap_along(after(weight, dv_all), "core", 1)

    parts = exchange(value_parts(tok, weight, other_weight, dv_all), CTX)
    spread_rows, values = middle(parts, dv_short)
    spread_rows = exchange(spread_rows, CTX)

    share = swap_along(weight_share(1, plane, tok, spread_rows), "core", 1)
    share = weight_share(0, plane, tok, spread_rows, share)
    values = after(values, share)
    share = exchange(share, ("ylo", "z"))
    d_query, dk_all, dk_short = dscores(scalars, queries, upstream, rotated_key_rows, values,
                                        all_keys, spread_rows)
    d_key, weight_grad = last(exchange(closing(share, dk_all), CTX), dk_short)
    return d_query, d_key, weight_grad


def solution(mesh):
    packs = mesh.shape["dp"]
    mesh = Mesh(mesh.devices.reshape(Y_LO, packs // (Y_LO * CORES), CORES, 2, N_CTX // 2), DP + CTX)
    rows = P(DP + CTX, None)
    return jax.shard_map(
        on_device,
        mesh=mesh,
        in_specs=(rows, rows, rows, rows, P(DP, None), rows, P(DP, None)),
        out_specs=(rows, rows, P(DP, None)),
        check_vma=False,
    )
```
